512 devices in a mesh: dp: 64 (over y_hi, z, core), group: 8 (over y_lo, x).
Axes of the slice: x: 4, y: 8 (y_hi: 4, y_lo: 2; y = y_hi * 2 + y_lo), z: 8, core: 2. Of those that a mesh axis runs over, the one named last changes fastest.
Arguments:
- activations: bfloat16 [1024, 6144], P('dp', 'group'), may hold values from -6 to 6
- out_grads: bfloat16 [1024, 6144], P('dp', 'group'), may hold values from -6 to 6
- counts: int32 [64], P('dp'), may hold values from 1 to 16, 768 in all
- owners: int32 [64], P('dp'), may hold values from 0 to 63, each once
- rotated_grad: bfloat16 [6144, 6144], P('dp'), may hold values from -6 to 6
- basis: bfloat16 [6144, 6144], P('dp', 'group'), may hold values from -0.078125 to 0.078125
- input_eigs: float32 [6144], P('group'), may hold values from 0.5 to 2
- output_eigs: float32 [6144], P('dp'), may hold values from 0.5 to 2
Outputs:
- cov_in: float32 [6144, 6144], P('group', 'dp')
- cov_out: float32 [6144, 6144], P('group', 'dp')
- preconditioned: float32 [6144, 6144], P('dp', 'group')
The draws below stay inside these ranges and needn't reach their ends.
Inputs may be any that keep to these rules, and one draw needn't show every extreme that they name: counts[i] live slots lead replica i's 16 slots; the counts sum to 768 and the largest equals 16. owners is a permutation.
All inputs are finite; a program needn't handle non-finite values. No bound on the sum of `counts` on one device may be relied on, other than what follows from the above.
Results may differ from the reference program's by a relative error of at most 0.0022.
Values may be sent and summed in bfloat16 or wider, within the bound.
No kernel may reach another device: no remote copies, remote signals or barrier semaphores. Data moves between devices by JAX's collectives and lax.ppermute only.
A program may use at most 64 MiB of HBM per device.

```python
import math
import jax
import jax.numpy as jnp
import numpy as np
from jax import lax

D = 6144
TOK_CAP = 16
SLOTS = 1024
SAMPLED = 768
GROWS = 6144
N_DP = 64


def level_of(rng, dims, shards, smallest, high):
    gain, own = 1.0, jax.random.fold_in(rng, 6)
    for axis_at, parts in shards:
        draws = jnp.exp(jax.random.uniform(jax.random.fold_in(own, axis_at), (parts,), jnp.float32, smallest / len(shards), high / len(shards)))
        gain = gain * jnp.repeat(draws, dims[axis_at] // parts).reshape([-1 if axis == axis_at else 1 for axis in range(len(dims))])
    return gain


def split_up(amount, total, limit, lean):
    weights = [(1 << 20) // math.isqrt(standing ** lean) + 1 for standing in range(2, amount + 1)]
    spare, given = total - limit - (amount - 1), [1] * (amount - 1)
    while spare > 0:
        movable = [i for i in range(amount - 1) if given[i] < limit]
        mass, budget = sum([weights[i] for i in movable]), spare
        for i in movable:
            more = min(limit - given[i], max(1, budget * weights[i] // mass), spare)
            given[i] = given[i] + more
            spare = spare - more
    return np.array([limit] + given)


def uneven(key, number_of, total, most, skew):
    if number_of == 2:
        one = jax.random.randint(key, (), max(1, total - most), min(most, total - 1) + 1)
        return jnp.stack([one, total - one])
    tallies = jnp.asarray(split_up(number_of, total, most, skew), jnp.int32)
    couples = (number_of - 1) // 2
    source_of, receiver = tallies[1:1 + 2 * couples:2], tallies[2:2 + 2 * couples:2]
    margin = jnp.minimum(source_of - 1, most - receiver)
    shifted = jax.random.randint(jax.random.fold_in(key, 1), (couples,), 0, 1 << 20) % (margin + 1)
    tallies = tallies.at[1:1 + 2 * couples:2].set(source_of - shifted).at[2:2 + 2 * couples:2].set(receiver + shifted)
    return tallies[jax.random.permutation(jax.random.fold_in(key, 2), number_of)]


def gaussian(own_key, dims, width, limit, pieces=(), held_as=jnp.bfloat16):
    drawn = width * jax.random.normal(own_key, dims, jnp.float32)
    if pieces:
        drawn = drawn * level_of(own_key, dims, pieces, -0.22, 0.18)
    return jnp.clip(drawn, -limit, limit).astype(held_as)


def setup_inputs(seed: int = 0) -> dict:
    splits = jax.random.split(jax.random.key(seed), 9)
    return {
        "activations": gaussian(splits[0], (SLOTS, D), 1.0, 6.0, ((0, 64), (1, 8))),
        "out_grads": gaussian(splits[1], (SLOTS, D), 1.0, 6.0, ((0, 64), (1, 8))),
        "counts": uneven(splits[2], N_DP, SAMPLED, TOK_CAP, 2).astype(jnp.int32),
        "owners": jax.random.permutation(splits[3], N_DP).astype(jnp.int32),
        "rotated_grad": gaussian(splits[4], (GROWS, D), 1.0, 6.0, ((0, 64),)),
        "basis": gaussian(splits[5], (D, D), D ** -0.5, 0.078125, ((0, 64), (1, 8))),
        "input_eigs": jnp.clip(jnp.exp(math.log(2.0) - 1.3862944 * jax.random.uniform(splits[6], (D,), jnp.float32) ** level_of(splits[6], (D,), ((0, 8),), -0.2, 0.2)), 0.5, 2.0),
        "output_eigs": jnp.clip(jnp.exp(math.log(2.0) - 1.3862944 * jax.random.uniform(splits[7], (GROWS,), jnp.float32) ** level_of(splits[7], (GROWS,), ((0, 64),), -0.2, 0.2)), 0.5, 2.0),
    }


DAMPING = 0.1


def covariance(kept, total):
    full = lax.dot_general(kept, kept, (((0,), (0,)), ((), ())), preferred_element_type=jnp.float32) / total
    return full


def reorder(full, owners):
    blocks = full.reshape(D, N_DP, D // N_DP)
    return blocks[:, owners, :].reshape(D, D)


def reference(activations, out_grads, counts, owners, rotated_grad, basis, input_eigs, output_eigs):
    positions = jnp.arange(SLOTS, dtype=jnp.int32)
    replica = positions // TOK_CAP
    is_live = (positions % TOK_CAP) < counts[replica]
    kept_in = jnp.where(is_live[:, None], activations, jnp.zeros_like(activations))
    kept_out = jnp.where(is_live[:, None], out_grads, jnp.zeros_like(out_grads))
    total = jnp.sum(counts.astype(jnp.float32))
    cov_in = reorder(covariance(kept_in, total), owners)
    cov_out = reorder(covariance(kept_out, total), owners)
    projected = jnp.dot(rotated_grad, basis, preferred_element_type=jnp.float32)
    scaled = (projected / (output_eigs[:, None] * input_eigs[None, :] + DAMPING)).astype(jnp.bfloat16)
    preconditioned = lax.dot_general(scaled, basis, (((1,), (1,)), ((), ())), preferred_element_type=jnp.float32)
    return cov_in, cov_out, preconditioned
```

```python
import jax
import jax.numpy as jnp
from jax import lax
from jax.sharding import Mesh, PartitionSpec as P

DAMPING = 0.1
SAMPLED = 768
DP = ("yh", "z", "core")
GROUP = ("yl", "x")


def shift(value, axis, by):
    size = lax.axis_size(axis)
    return lax.ppermute(value, axis, [((i + by) % size, i) for i in range(size)])


def gather_y(block):
    return [block] + [shift(block, "yh", k) for k in range(1, 4)]


def gather_z(block):
    chunks = [block]
    up = down = block
    for step in range(4):
        up = shift(up, "z", 1)
        chunks.append(up)
        if step < 3:
            down = shift(down, "z", -1)
            chunks.append(down)
    return chunks


def shards(activations, out_grads, counts, owners, rotated_grad, basis, input_eigs, output_eigs):
    slots, width = activations.shape
    owned_width = basis.shape[0]
    blocks_per = width // owned_width
    group_count = lax.axis_size("yl") * lax.axis_size("x")
    full_basis = lax.all_gather(basis, DP, axis=0, tiled=True)

    is_live = lax.broadcasted_iota(jnp.int32, (slots, 1), 0) < counts[0]
    kept = jnp.stack([jnp.where(is_live, v, jnp.zeros_like(v)) for v in (activations, out_grads)])
    kept = jnp.concatenate(gather_y(kept), axis=1)
    kept = jnp.concatenate(gather_z(kept), axis=1)
    both = jnp.concatenate([kept, shift(kept, "core", 1)], axis=1)
    samples = both.shape[1]
    owner_idx = owners[0]
    offset = owner_idx % blocks_per * owned_width
    owned = lax.dynamic_slice_in_dim(both, offset, owned_width, 2)
    pieces = owned.reshape(group_count, 2 * samples // group_count, owned_width)
    pieces = lax.all_to_all(pieces, GROUP, 0, 0, tiled=True)
    piece = lax.dynamic_index_in_dim(pieces, owner_idx // blocks_per, 0, keepdims=False)
    spread = jnp.broadcast_to(piece[None], pieces.shape)
    owned = lax.all_to_all(spread, GROUP, 0, 0, tiled=True).reshape(2, samples, owned_width)
    contract_rows = (((0,), (0,)), ((), ()))
    cov_in, cov_out = (
        lax.dot_general(both[k], owned[k], contract_rows, preferred_element_type=jnp.float32)
        / jnp.float32(SAMPLED)
        for k in range(2)
    )

    contract_cols = (((1,), (1,)), ((), ()))
    denominator = output_eigs[:, None] * input_eigs[None, :] + DAMPING
    projected = jnp.dot(rotated_grad, full_basis, preferred_element_type=jnp.float32)
    scaled = (projected / denominator).astype(jnp.bfloat16)
    wide = full_basis.reshape(group_count, width, width)
    terms = lax.dot_general(
        wide, scaled, (((2,), (1,)), ((), ())), preferred_element_type=jnp.float32
    )
    terms = jnp.swapaxes(terms, 1, 2)
    terms = lax.all_to_all(terms, GROUP, 0, 0, tiled=True)
    preconditioned = jnp.sum(terms, axis=0)
    return (cov_in, cov_out, preconditioned)


def solution(mesh):
    devices = mesh.devices.reshape(4, 8, 2, 2, 4)
    fine = Mesh(devices, DP + GROUP)
    placed = (
        P(DP, GROUP),
        P(DP, GROUP),
        P(DP),
        P(DP),
        P(DP, None),
        P(DP, GROUP),
        P(GROUP),
        P(DP),
    )
    return jax.shard_map(
        shards,
        mesh=fine,
        in_specs=placed,
        out_specs=(P(GROUP, DP), P(GROUP, DP), P(DP, GROUP)),
        check_vma=False,
    )
```

```python
import functools

import jax
import jax.numpy as jnp
from jax import lax
from jax.experimental import pallas as pl
from jax.experimental.pallas import tpu as pltpu
from jax.sharding import Mesh, PartitionSpec as P

DAMPING = 0.1
SAMPLED = 768
DP = ("yh", "z", "core")
GROUP = ("yl", "x")
GATHERED = 384


def shift(value, axis, by):
    size = lax.axis_size(axis)
    return lax.ppermute(value, axis, [((i + by) % size, i) for i in range(size)])


def spread(block, axis):
    size = lax.axis_size(axis)
    return lax.all_to_all(jnp.broadcast_to(block[None], (size,) + block.shape), axis, 0, 0, tiled=True)


def ring_z(block):
    chunks = [(0, block)]
    up = down = block
    for step in range(1, 5):
        up = shift(up, "z", 1)
        chunks.append((step, up))
        if step < 4:
            down = shift(down, "z", -1)
            chunks.append((-step, down))
    return chunks


def precondition_kernel(
    near, place, gathered, gathered_other, *refs
):
    ring_refs, (grad, in_eigs, out_eigs, terms, basis, sems) = refs[:-6], refs[-6:]
    z, core = place[0], place[1]
    copies = []

    def bring(src, z_at, core_at, start, width):
        copy = pltpu.make_async_copy(
            src, basis.at[:, z_at, core_at, :, pl.ds(start, width)], sems.at[len(copies)]
        )
        copy.start()
        copies.append(copy)

    left = gathered.shape[-1]
    right = grad.shape[1] // 8 - left
    for k in range(8):
        bring(gathered.at[k], k, core, 0, left)
        bring(gathered_other.at[k], k, 1 - core, 0, left)
    half = len(ring_refs) // 2
    for side in range(2):
        at = 0
        for ref in ring_refs[side * half : (side + 1) * half]:
            for k in range(ref.shape[0]):
                z_at = lax.rem(z + (near[at] + 8), 8)
                bring(ref.at[k], z_at, core if side == 0 else 1 - core, left, right)
                at += 1
    for copy in copies:
        copy.wait()

    width = left + right
    projected = jnp.zeros((grad.shape[0], width), jnp.float32)
    for k in range(8):
        rows = basis[k // 2, (k % 2) * 4 : (k % 2) * 4 + 4].reshape(width, width)
        projected += jnp.dot(
            grad[:, k * width : (k + 1) * width], rows, preferred_element_type=jnp.float32
        )
    denominator = out_eigs[...] * in_eigs[...] + DAMPING
    scaled = (projected / denominator).astype(jnp.bfloat16)
    for k in range(8):
        rows = basis[k // 2, (k % 2) * 4 : (k % 2) * 4 + 4].reshape(width, width)
        terms[k] = lax.dot_general(
            scaled, rows, (((1,), (1,)), ((), ())), preferred_element_type=jnp.float32
        )


def precondition(near, gathered, gathered_other, ring, ring_other, grad, in_eigs, out_eigs):
    place = jnp.stack([lax.axis_index("z"), lax.axis_index("core")]).astype(jnp.int32)
    rows = grad.shape[0]
    width = in_eigs.shape[0]
    anywhere = pl.BlockSpec(memory_space=pl.ANY)
    vmem = pl.BlockSpec(memory_space=pltpu.VMEM)
    return pl.pallas_call(
        functools.partial(precondition_kernel, near),
        out_shape=jax.ShapeDtypeStruct((8, rows, width), jnp.float32),
        in_specs=[pl.BlockSpec(memory_space=pltpu.SMEM)]
        + [anywhere] * (2 + len(ring) + len(ring_other))
        + [vmem] * 3,
        out_specs=vmem,
        scratch_shapes=[
            pltpu.VMEM((4, 8, 2, rows, width), jnp.bfloat16),
            pltpu.SemaphoreType.DMA((32,)),
        ],
        compiler_params=pltpu.CompilerParams(vmem_limit_bytes=36 << 20),
        cost_estimate=pl.CostEstimate(
            flops=4 * rows * 8 * width * width, bytes_accessed=24 * width * width, transcendentals=0
        ),
    )(place, gathered, gathered_other, *ring, *ring_other, grad, in_eigs[None, :], out_eigs[:, None])


def shards(activations, out_grads, counts, owners, rotated_grad, basis, input_eigs, output_eigs):
    slots, width = activations.shape
    owned_width = basis.shape[0]
    blocks_per = width // owned_width
    group_count = lax.axis_size("yl") * lax.axis_size("x")

    first = spread(basis[:, :GATHERED], "yh")
    second = spread(basis[:, GATHERED:], "yh")
    gathered = lax.all_gather(first, "z", axis=0)
    gathered_other = shift(gathered, "core", 1)
    chunks = ring_z(second)
    near = [distance for distance, _ in chunks]
    early = jnp.stack([value for _, value in chunks[:5]])
    late = jnp.stack([value for _, value in chunks[5:]])
    ring = [early, late]
    ring_other = [shift(v, "core", 1) for v in ring]

    is_live = lax.broadcasted_iota(jnp.int32, (slots, 1), 0) < counts[0]
    kept = jnp.stack([jnp.where(is_live, v, jnp.zeros_like(v)) for v in (activations, out_grads)])
    kept = spread(spread(kept, "z"), "yh")
    kept = jnp.moveaxis(kept, 2, 0).reshape(2, -1, width)
    both = jnp.concatenate([kept, shift(kept, "core", 1)], axis=1)
    samples = both.shape[1]
    owner_idx = owners[0]
    offset = owner_idx % blocks_per * owned_width
    owned = lax.dynamic_slice_in_dim(both, offset, owned_width, 2)
    pieces = owned.reshape(group_count, 2 * samples // group_count, owned_width)
    pieces = lax.all_to_all(pieces, GROUP, 0, 0, tiled=True)
    piece = lax.dynamic_index_in_dim(pieces, owner_idx // blocks_per, 0, keepdims=False)
    owned = spread(piece, GROUP).reshape(2, samples, owned_width)
    contract_rows = (((0,), (0,)), ((), ()))
    cov_in, cov_out = (
        lax.dot_general(both[k], owned[k], contract_rows, preferred_element_type=jnp.float32)
        / jnp.float32(SAMPLED)
        for k in range(2)
    )

    terms = precondition(
        near, gathered, gathered_other, ring, ring_other, rotated_grad, input_eigs, output_eigs
    )
    terms = lax.all_to_all(terms, GROUP, 0, 0, tiled=True)
    preconditioned = jnp.sum(terms, axis=0)
    return (cov_in, cov_out, preconditioned)


def solution(mesh):
    devices = mesh.devices.reshape(4, 8, 2, 2, 4)
    fine = Mesh(devices, DP + GROUP)
    placed = (
        P(DP, GROUP),
        P(DP, GROUP),
        P(DP),
        P(DP),
        P(DP, None),
        P(DP, GROUP),
        P(GROUP),
        P(DP),
    )
    return jax.shard_map(
        shards,
        mesh=fine,
        in_specs=placed,
        out_specs=(P(GROUP, DP), P(GROUP, DP), P(DP, GROUP)),
        check_vma=False,
    )
```

```python
import jax
import jax.numpy as jnp
from jax import lax
from jax.experimental import pallas as pl
from jax.experimental.pallas import tpu as pltpu
from jax.sharding import Mesh, PartitionSpec as P

DAMPING = 0.1
SAMPLED = 768
DP = ("yh", "z", "core")
GROUP = ("yl", "x")
GATHERED, RINGED = 512, 256
NEAR = ((0, 1, -1), (2, -2), (3, -3, 4))


def shift(value, axis, by):
    size = lax.axis_size(axis)
    return lax.ppermute(value, axis, [((i + by) % size, i) for i in range(size)])


def others(block, axis):
    return [shift(block, axis, k) for k in range(1, lax.axis_size(axis))]


def spread(block, axis):
    size = lax.axis_size(axis)
    return lax.all_to_all(jnp.broadcast_to(block[None], (size,) + block.shape), axis, 0, 0, tiled=True)


def after(value, *others):
    return lax.optimization_barrier((value,) + others)[0]


def precondition_kernel(place, *refs):
    gathered, ring = refs[0:2], (refs[2:5], refs[5:8])
    grad, in_eigs, out_eigs, terms, basis, sems = refs[8:]
    z, core = place[0], place[1]
    width = basis.shape[-1]
    copies = []

    def bring(src, target):
        copy = pltpu.make_async_copy(src, target, sems.at[len(copies)])
        copy.start()
        copies.append(copy)

    for side in range(2):
        at = core if side == 0 else 1 - core
        columns = pl.ds(0, GATHERED)
        for k in range(8):
            bring(gathered[side].at[k], basis.at[:, k, at, :, columns])
        columns = pl.ds(GATHERED, RINGED)
        for ref, distances in zip(ring[side], NEAR):
            for k, distance in enumerate(distances):
                bring(ref.at[k], basis.at[:, lax.rem(z + (distance + 8), 8), at, :, columns])
    for copy in copies:
        copy.wait()

    projected = jnp.zeros((grad.shape[0], width), jnp.float32)
    for k in range(8):
        rows = basis[k // 2, (k % 2) * 4 : (k % 2) * 4 + 4].reshape(width, width)
        projected += jnp.dot(
            grad[:, k * width : (k + 1) * width], rows, preferred_element_type=jnp.float32
        )
    denominator = out_eigs[...] * in_eigs[...] + DAMPING
    scaled = (projected / denominator).astype(jnp.bfloat16)
    for k in range(8):
        rows = basis[k // 2, (k % 2) * 4 : (k % 2) * 4 + 4].reshape(width, width)
        terms[k] = lax.dot_general(
            scaled, rows, (((1,), (1,)), ((), ())), preferred_element_type=jnp.float32
        )


def precondition(pieces, grad, in_eigs, out_eigs):
    place = jnp.stack([lax.axis_index("z"), lax.axis_index("core")]).astype(jnp.int32)
    rows = grad.shape[0]
    width = in_eigs.shape[0]
    vmem = pl.BlockSpec(memory_space=pltpu.VMEM)
    return pl.pallas_call(
        precondition_kernel,
        out_shape=jax.ShapeDtypeStruct((8, rows, width), jnp.float32),
        in_specs=[pl.BlockSpec(memory_space=pltpu.SMEM)]
        + [pl.BlockSpec(memory_space=pl.ANY)] * len(pieces)
        + [vmem] * 3,
        out_specs=vmem,
        scratch_shapes=[
            pltpu.VMEM((4, 8, 2, rows, width), jnp.bfloat16),
            pltpu.SemaphoreType.DMA((32,)),
        ],
        compiler_params=pltpu.CompilerParams(vmem_limit_bytes=36 << 20),
        cost_estimate=pl.CostEstimate(
            flops=4 * rows * 8 * width * width, bytes_accessed=24 * width * width, transcendentals=0
        ),
    )(place, *pieces, grad, in_eigs[None, :], out_eigs[:, None])


def shards(activations, out_grads, counts, owners, rotated_grad, basis, input_eigs, output_eigs):
    slots, width = activations.shape
    owned_width = basis.shape[0]
    blocks_per = width // owned_width
    group_count = lax.axis_size("yl") * lax.axis_size("x")

    is_live = lax.broadcasted_iota(jnp.int32, (slots, 1), 0) < counts[0]
    kept = jnp.concatenate([jnp.where(is_live, v, jnp.zeros_like(v)) for v in (activations, out_grads)])
    first = spread(basis[:, :GATHERED], "yh")
    second, *near = lax.optimization_barrier((spread(basis[:, GATHERED:], "yh"), *others(kept, "z")))
    gathered = lax.all_gather(first, "z", axis=0)
    up1, down1 = lax.optimization_barrier((shift(second, "z", 1), shift(second, "z", -1)))
    up2, down2 = lax.optimization_barrier((shift(up1, "z", 1), shift(down1, "z", -1)))
    up3, down3 = lax.optimization_barrier((shift(up2, "z", 1), shift(down2, "z", -1)))
    up4 = shift(up3, "z", 1)
    ring = [jnp.stack(group) for group in ((second, up1, down1), (up2, down2), (up3, down3, up4))]
    gathered = after(gathered, up4)

    kept = jnp.concatenate([kept] + near)
    kept = jnp.concatenate([kept] + others(kept, "yh"))
    kept = after(kept, up4).reshape(-1, 2, slots, width)
    kept = jnp.moveaxis(kept, 1, 0).reshape(2, -1, width)
    both = jnp.concatenate([kept, shift(kept, "core", 1)], axis=1)
    samples = both.shape[1]
    owner_idx = owners[0]
    offset = owner_idx % blocks_per * owned_width
    owned = lax.dynamic_slice_in_dim(both, offset, owned_width, 2)
    pieces = owned.reshape(group_count, 2 * samples // group_count, owned_width)
    pieces = lax.all_to_all(pieces, GROUP, 0, 0, tiled=True)
    piece = lax.dynamic_index_in_dim(pieces, owner_idx // blocks_per, 0, keepdims=False)
    owned = spread(piece, GROUP).reshape(2, samples, owned_width)
    contract_rows = (((0,), (0,)), ((), ()))
    cov_in, cov_out = (
        lax.dot_general(both[k], owned[k], contract_rows, preferred_element_type=jnp.float32)
        / jnp.float32(SAMPLED)
        for k in range(2)
    )

    pieces = [gathered, shift(gathered, "core", 1)]
    pieces += ring + [shift(group, "core", 1) for group in ring]
    terms = precondition(pieces, rotated_grad, input_eigs, output_eigs)
    terms = lax.all_to_all(terms, GROUP, 0, 0, tiled=True)
    preconditioned = jnp.sum(terms, axis=0)
    return (cov_in, cov_out, preconditioned)


def solution(mesh):
    devices = mesh.devices.reshape(4, 8, 2, 2, 4)
    fine = Mesh(devices, DP + GROUP)
    placed = (
        P(DP, GROUP),
        P(DP, GROUP),
        P(DP),
        P(DP),
        P(DP, None),
        P(DP, GROUP),
        P(GROUP),
        P(DP),
    )
    return jax.shard_map(
        shards,
        mesh=fine,
        in_specs=placed,
        out_specs=(P(GROUP, DP), P(GROUP, DP), P(DP, GROUP)),
        check_vma=False,
    )
```

```python
import jax
import jax.numpy as jnp
from jax import lax
from jax.experimental import pallas as pl
from jax.experimental.pallas import tpu as pltpu
from jax.sharding import Mesh, PartitionSpec as P

DAMPING = 0.1
SAMPLED = 768
DP = ("yh", "z", "core")
GROUP = ("yl", "x")


def shift(value, axis, by):
    size = lax.axis_size(axis)
    return lax.ppermute(value, axis, [((i + by) % size, i) for i in range(size)])


def spread(block, axis):
    size = lax.axis_size(axis)
    return lax.all_to_all(jnp.broadcast_to(block[None], (size,) + block.shape), axis, 0, 0, tiled=True)


def gather_z(block):
    chunks = [block]
    up = down = block
    for step in range(4):
        up = shift(up, "z", 1)
        chunks.append(up)
        if step < 3:
            down = shift(down, "z", -1)
            chunks.append(down)
    return chunks


def precondition_kernel(place, own, other, grad, in_eigs, out_eigs, terms, basis, sems):
    core = place[0]
    rows, width = in_eigs.shape[1], basis.shape[-1]
    steps = basis.shape[0] * 2
    copies = []
    for k in range(steps):
        y, zs = k // 2, pl.ds(k % 2 * 4, 4)
        copies.append(
            [
                pltpu.make_async_copy(src.at[zs, y], basis.at[y, zs, at], sems.at[2 * k + side])
                for side, (src, at) in enumerate(((own, core), (other, 1 - core)))
            ]
        )
    for pair in copies:
        for copy in pair:
            copy.start()

    def block(k):
        return basis[k // 2, k % 2 * 4 : k % 2 * 4 + 4].reshape(rows, width)

    projected = jnp.zeros((grad.shape[0], width), jnp.float32)
    for k in range(steps):
        for copy in copies[k]:
            copy.wait()
        projected += jnp.dot(
            grad[:, k * rows : (k + 1) * rows], block(k), preferred_element_type=jnp.float32
        )
    denominator = out_eigs[...] * in_eigs[...] + DAMPING
    scaled = (projected / denominator).astype(jnp.bfloat16)
    for k in range(steps):
        terms[k] = lax.dot_general(
            scaled, block(k), (((1,), (1,)), ((), ())), preferred_element_type=jnp.float32
        )


def precondition(own, other, grad, in_eigs, out_eigs):
    place = lax.axis_index("core").astype(jnp.int32)[None]
    rows = grad.shape[0]
    width = in_eigs.shape[0]
    anywhere = pl.BlockSpec(memory_space=pl.ANY)
    vmem = pl.BlockSpec(memory_space=pltpu.VMEM)
    return pl.pallas_call(
        precondition_kernel,
        out_shape=jax.ShapeDtypeStruct((8, rows, width), jnp.float32),
        in_specs=[pl.BlockSpec(memory_space=pltpu.SMEM), anywhere, anywhere, vmem, vmem, vmem],
        out_specs=vmem,
        scratch_shapes=[
            pltpu.VMEM((4, 8, 2, rows, width), jnp.bfloat16),
            pltpu.SemaphoreType.DMA((16,)),
        ],
        compiler_params=pltpu.CompilerParams(vmem_limit_bytes=36 << 20),
        cost_estimate=pl.CostEstimate(
            flops=4 * rows * 8 * width * width, bytes_accessed=24 * width * width, transcendentals=0
        ),
    )(place, own, other, grad, in_eigs[None, :], out_eigs[:, None])


def shards(activations, out_grads, counts, owners, rotated_grad, basis, input_eigs, output_eigs):
    slots, width = activations.shape
    owned_width = basis.shape[0]
    blocks_per = width // owned_width
    group_count = lax.axis_size("yl") * lax.axis_size("x")
    is_live = lax.broadcasted_iota(jnp.int32, (slots, 1), 0) < counts[0]
    kept = [jnp.where(is_live, v, jnp.zeros_like(v)) for v in (activations, out_grads)]
    column = spread(jnp.concatenate([basis] + kept), "yh")
    own = lax.all_gather(column[:, :owned_width], "z", axis=0)
    kept = column[:, owned_width:].reshape(-1, 2, slots, width)
    kept = jnp.moveaxis(kept, 1, 0).reshape(2, -1, width)
    kept = jnp.concatenate(gather_z(kept), axis=1)
    both = jnp.concatenate([kept, shift(kept, "core", 1)], axis=1)
    samples = both.shape[1]
    owner_idx = owners[0]
    offset = owner_idx % blocks_per * owned_width
    owned = lax.dynamic_slice_in_dim(both, offset, owned_width, 2)
    pieces = owned.reshape(group_count, 2 * samples // group_count, owned_width)
    pieces = lax.all_to_all(pieces, GROUP, 0, 0, tiled=True)
    piece = lax.dynamic_index_in_dim(pieces, owner_idx // blocks_per, 0, keepdims=False)
    own, piece = lax.optimization_barrier((own, piece))
    owned = spread(piece, GROUP).reshape(2, samples, owned_width)
    contract_rows = (((0,), (0,)), ((), ()))
    cov_in, cov_out = (
        lax.dot_general(both[k], owned[k], contract_rows, preferred_element_type=jnp.float32)
        / jnp.float32(SAMPLED)
        for k in range(2)
    )

    other = shift(own, "core", 1)
    terms = precondition(own, other, rotated_grad, input_eigs, output_eigs)
    terms = lax.all_to_all(terms, GROUP, 0, 0, tiled=True)
    preconditioned = jnp.sum(terms, axis=0)
    return (cov_in, cov_out, preconditioned)


def solution(mesh):
    devices = mesh.devices.reshape(4, 8, 2, 2, 4)
    fine = Mesh(devices, DP + GROUP)
    placed = (
        P(DP, GROUP),
        P(DP, GROUP),
        P(DP),
        P(DP),
        P(DP, None),
        P(DP, GROUP),
        P(GROUP),
        P(DP),
    )
    return jax.shard_map(
        shards,
        mesh=fine,
        in_specs=placed,
        out_specs=(P(GROUP, DP), P(GROUP, DP), P(DP, GROUP)),
        check_vma=False,
    )
```

```python
import jax
import jax.numpy as jnp
from jax import lax
from jax.experimental import pallas as pl
from jax.experimental.pallas import tpu as pltpu
from jax.sharding import Mesh, PartitionSpec as P

DAMPING = 0.1
SAMPLED = 768
DP = ("yh", "z", "core")
GROUP = ("yl", "x")


def shift(value, axis, by):
    size = lax.axis_size(axis)
    return lax.ppermute(value, axis, [((i + by) % size, i) for i in range(size)])


def spread(block, axis):
    size = lax.axis_size(axis)
    return lax.all_to_all(jnp.broadcast_to(block[None], (size,) + block.shape), axis, 0, 0, tiled=True)


def precondition_kernel(place, own, other, grad, in_eigs, out_eigs, terms, basis, sems):
    core = place[0]
    rows, width = in_eigs.shape[1], basis.shape[-1]
    steps = basis.shape[0] * 2
    copies = []
    for k in range(steps):
        y, zs = k // 2, pl.ds(k % 2 * 4, 4)
        copies.append(
            [
                pltpu.make_async_copy(src.at[zs, y], basis.at[y, zs, at], sems.at[2 * k + side])
                for side, (src, at) in enumerate(((own, core), (other, 1 - core)))
            ]
        )
    for pair in copies:
        for copy in pair:
            copy.start()

    def block(k):
        return basis[k // 2, k % 2 * 4 : k % 2 * 4 + 4].reshape(rows, width)

    projected = jnp.zeros((grad.shape[0], width), jnp.float32)
    for k in range(steps):
        for copy in copies[k]:
            copy.wait()
        projected += jnp.dot(
            grad[:, k * rows : (k + 1) * rows], block(k), preferred_element_type=jnp.float32
        )
    denominator = out_eigs[...] * in_eigs[...] + DAMPING
    scaled = (projected / denominator).astype(jnp.bfloat16)
    for k in range(steps):
        terms[k] = lax.dot_general(
            scaled, block(k), (((1,), (1,)), ((), ())), preferred_element_type=jnp.float32
        )


def precondition(own, other, grad, in_eigs, out_eigs):
    place = lax.axis_index("core").astype(jnp.int32)[None]
    rows = grad.shape[0]
    width = in_eigs.shape[0]
    anywhere = pl.BlockSpec(memory_space=pl.ANY)
    vmem = pl.BlockSpec(memory_space=pltpu.VMEM)
    return pl.pallas_call(
        precondition_kernel,
        out_shape=jax.ShapeDtypeStruct((8, rows, width), jnp.float32),
        in_specs=[pl.BlockSpec(memory_space=pltpu.SMEM), anywhere, anywhere, vmem, vmem, vmem],
        out_specs=vmem,
        scratch_shapes=[
            pltpu.VMEM((4, 8, 2, rows, width), jnp.bfloat16),
            pltpu.SemaphoreType.DMA((16,)),
        ],
        compiler_params=pltpu.CompilerParams(vmem_limit_bytes=36 << 20),
        cost_estimate=pl.CostEstimate(
            flops=4 * rows * 8 * width * width, bytes_accessed=24 * width * width, transcendentals=0
        ),
    )(place, own, other, grad, in_eigs[None, :], out_eigs[:, None])


def shards(activations, out_grads, counts, owners, rotated_grad, basis, input_eigs, output_eigs):
    slots, width = activations.shape
    owned_width = basis.shape[0]
    blocks_per = width // owned_width
    group_count = lax.axis_size("yl") * lax.axis_size("x")
    is_live = lax.broadcasted_iota(jnp.int32, (slots, 1), 0) < counts[0]
    kept = jnp.concatenate([jnp.where(is_live, v, jnp.zeros_like(v)) for v in (activations, out_grads)])
    column, kept = lax.optimization_barrier((spread(basis, "yh"), kept))
    own = lax.all_gather(column, "z", axis=0)
    kept = spread(spread(kept, "z").reshape(-1, width), "yh")
    kept = jnp.moveaxis(kept.reshape(-1, 2, slots, width), 1, 0).reshape(2, -1, width)
    both = jnp.concatenate([kept, shift(kept, "core", 1)], axis=1)
    samples = both.shape[1]
    owner_idx = owners[0]
    offset = owner_idx % blocks_per * owned_width
    owned = lax.dynamic_slice_in_dim(both, offset, owned_width, 2)
    pieces = owned.reshape(group_count, 2 * samples // group_count, owned_width)
    pieces = lax.all_to_all(pieces, GROUP, 0, 0, tiled=True)
    piece = lax.dynamic_index_in_dim(pieces, owner_idx // blocks_per, 0, keepdims=False)
    own, piece = lax.optimization_barrier((own, piece))
    owned = spread(piece, GROUP).reshape(2, samples, owned_width)
    contract_rows = (((0,), (0,)), ((), ()))
    cov_in, cov_out = (
        lax.dot_general(both[k], owned[k], contract_rows, preferred_element_type=jnp.float32)
        / jnp.float32(SAMPLED)
        for k in range(2)
    )

    other = shift(own, "core", 1)
    terms = precondition(own, other, rotated_grad, input_eigs, output_eigs)
    terms = lax.all_to_all(terms, GROUP, 0, 0, tiled=True)
    preconditioned = jnp.sum(terms, axis=0)
    return (cov_in, cov_out, preconditioned)


def solution(mesh):
    devices = mesh.devices.reshape(4, 8, 2, 2, 4)
    fine = Mesh(devices, DP + GROUP)
    placed = (
        P(DP, GROUP),
        P(DP, GROUP),
        P(DP),
        P(DP),
        P(DP, None),
        P(DP, GROUP),
        P(GROUP),
        P(DP),
    )
    return jax.shard_map(
        shards,
        mesh=fine,
        in_specs=placed,
        out_specs=(P(GROUP, DP), P(GROUP, DP), P(DP, GROUP)),
        check_vma=False,
    )
```

```python
import jax
import jax.numpy as jnp
from jax import lax
from jax.experimental import pallas as pl
from jax.experimental.pallas import tpu as pltpu
from jax.sharding import Mesh, PartitionSpec as P

DAMPING = 0.1
SAMPLED = 768
DP = ("yh", "z", "core")
GROUP = ("yl", "x")


def shift(value, axis, by):
    size = lax.axis_size(axis)
    return lax.ppermute(value, axis, [((i + by) % size, i) for i in range(size)])


def spread(block, axis):
    size = lax.axis_size(axis)
    return lax.all_to_all(jnp.broadcast_to(block[None], (size,) + block.shape), axis, 0, 0, tiled=True)


def precondition_kernel(place, own, other, grad, in_eigs, out_eigs, terms, basis, sems):
    core = place[0]
    rows, width = in_eigs.shape[1], basis.shape[-1]
    steps = basis.shape[0] * 2
    copies = []
    for k in range(steps):
        y, zs = k // 2, pl.ds(k % 2 * 4, 4)
        copies.append(
            [
                pltpu.make_async_copy(src.at[zs, y], basis.at[y, zs, at], sems.at[2 * k + side])
                for side, (src, at) in enumerate(((own, core), (other, 1 - core)))
            ]
        )
    for pair in copies:
        for copy in pair:
            copy.start()

    def block(k):
        return basis[k // 2, k % 2 * 4 : k % 2 * 4 + 4].reshape(rows, width)

    projected = jnp.zeros((grad.shape[0], width), jnp.float32)
    for k in range(steps):
        for copy in copies[k]:
            copy.wait()
        projected += jnp.dot(
            grad[:, k * rows : (k + 1) * rows], block(k), preferred_element_type=jnp.float32
        )
    denominator = out_eigs[...] * in_eigs[...] + DAMPING
    scaled = (projected / denominator).astype(jnp.bfloat16)
    for k in range(steps):
        terms[k] = lax.dot_general(
            scaled, block(k), (((1,), (1,)), ((), ())), preferred_element_type=jnp.float32
        )


def precondition(own, other, grad, in_eigs, out_eigs):
    place = lax.axis_index("core").astype(jnp.int32)[None]
    rows = grad.shape[0]
    width = in_eigs.shape[0]
    anywhere = pl.BlockSpec(memory_space=pl.ANY)
    vmem = pl.BlockSpec(memory_space=pltpu.VMEM)
    return pl.pallas_call(
        precondition_kernel,
        out_shape=jax.ShapeDtypeStruct((8, rows, width), jnp.float32),
        in_specs=[pl.BlockSpec(memory_space=pltpu.SMEM), anywhere, anywhere, vmem, vmem, vmem],
        out_specs=vmem,
        scratch_shapes=[
            pltpu.VMEM((4, 8, 2, rows, width), jnp.bfloat16),
            pltpu.SemaphoreType.DMA((16,)),
        ],
        compiler_params=pltpu.CompilerParams(vmem_limit_bytes=36 << 20),
        cost_estimate=pl.CostEstimate(
            flops=4 * rows * 8 * width * width, bytes_accessed=24 * width * width, transcendentals=0
        ),
    )(place, own, other, grad, in_eigs[None, :], out_eigs[:, None])


def shards(activations, out_grads, counts, owners, rotated_grad, basis, input_eigs, output_eigs):
    slots, width = activations.shape
    owned_width = basis.shape[0]
    blocks_per = width // owned_width
    group_count = lax.axis_size("yl") * lax.axis_size("x")
    is_live = lax.broadcasted_iota(jnp.int32, (slots, 1), 0) < counts[0]
    kept_in, kept_out = (jnp.where(is_live, v, jnp.zeros_like(v)) for v in (activations, out_grads))
    column, kept_out = lax.optimization_barrier(
        (spread(jnp.concatenate([basis, kept_in]), "yh"), kept_out)
    )
    own = lax.all_gather(column[:, :owned_width], "z", axis=0)
    kept_in, kept_out = lax.optimization_barrier((column[:, owned_width:], spread(kept_out, "z")))
    kept_out = spread(kept_out.reshape(-1, width), "yh").reshape(-1, width)
    kept_in = lax.all_gather(kept_in.reshape(-1, width), "z", axis=0, tiled=True)
    kept = jnp.stack([kept_in, kept_out])
    both = jnp.concatenate([kept, shift(kept, "core", 1)], axis=1)
    samples = both.shape[1]
    owner_idx = owners[0]
    offset = owner_idx % blocks_per * owned_width
    owned = lax.dynamic_slice_in_dim(both, offset, owned_width, 2)
    pieces = owned.reshape(group_count, 2 * samples // group_count, owned_width)
    pieces = lax.all_to_all(pieces, GROUP, 0, 0, tiled=True)
    piece = lax.dynamic_index_in_dim(pieces, owner_idx // blocks_per, 0, keepdims=False)
    own, piece = lax.optimization_barrier((own, piece))
    owned = spread(piece, GROUP).reshape(2, samples, owned_width)
    contract_rows = (((0,), (0,)), ((), ()))
    cov_in, cov_out = (
        lax.dot_general(both[k], owned[k], contract_rows, preferred_element_type=jnp.float32)
        / jnp.float32(SAMPLED)
        for k in range(2)
    )

    other = shift(own, "core", 1)
    terms = precondition(own, other, rotated_grad, input_eigs, output_eigs)
    terms = lax.all_to_all(terms, GROUP, 0, 0, tiled=True)
    preconditioned = jnp.sum(terms, axis=0)
    return (cov_in, cov_out, preconditioned)


def solution(mesh):
    devices = mesh.devices.reshape(4, 8, 2, 2, 4)
    fine = Mesh(devices, DP + GROUP)
    placed = (
        P(DP, GROUP),
        P(DP, GROUP),
        P(DP),
        P(DP),
        P(DP, None),
        P(DP, GROUP),
        P(GROUP),
        P(DP),
    )
    return jax.shard_map(
        shards,
        mesh=fine,
        in_specs=placed,
        out_specs=(P(GROUP, DP), P(GROUP, DP), P(DP, GROUP)),
        check_vma=False,
    )
```

```python
import jax
import jax.numpy as jnp
from jax import lax
from jax.experimental import pallas as pl
from jax.experimental.pallas import tpu as pltpu
from jax.sharding import Mesh, PartitionSpec as P

DAMPING = 0.1
SAMPLED = 768
DP = ("yh", "z", "core")
GROUP = ("yl", "x")


def shift(value, axis, by):
    size = lax.axis_size(axis)
    return lax.ppermute(value, axis, [((i + by) % size, i) for i in range(size)])


def spread(block, axis):
    size = lax.axis_size(axis)
    return lax.all_to_all(jnp.broadcast_to(block[None], (size,) + block.shape), axis, 0, 0, tiled=True)


def precondition_kernel(place, own, other, grad, in_eigs, out_eigs, terms, kept, basis, sems):
    core, member = place[0], place[1]
    rows, width = in_eigs.shape[1], basis.shape[-1]
    steps = basis.shape[0] * 2
    copies = []
    for k in range(steps):
        y, zs = k // 2, pl.ds(k % 2 * 4, 4)
        copies.append(
            [
                pltpu.make_async_copy(src.at[zs, y], basis.at[y, zs, at], sems.at[2 * k + side])
                for side, (src, at) in enumerate(((own, core), (other, 1 - core)))
            ]
        )
    for pair in copies:
        for copy in pair:
            copy.start()

    def block(k):
        return basis[k // 2, k % 2 * 4 : k % 2 * 4 + 4].reshape(rows, width)

    projected = jnp.zeros((grad.shape[0], width), jnp.float32)
    for k in range(steps):
        for copy in copies[k]:
            copy.wait()
        projected += jnp.dot(
            grad[:, k * rows : (k + 1) * rows], block(k), preferred_element_type=jnp.float32
        )
    denominator = out_eigs[...] * in_eigs[...] + DAMPING
    scaled = (projected / denominator).astype(jnp.bfloat16)
    for k in range(steps):
        share = lax.dot_general(
            scaled, block(k), (((1,), (1,)), ((), ())), preferred_element_type=jnp.float32
        )

        @pl.when(member == k)
        def _():
            kept[...] = share

        terms[k] = jnp.where(member == k, 0.0, share).astype(terms.dtype)


def precondition(own, other, grad, in_eigs, out_eigs):
    place = jnp.stack([lax.axis_index("core"), lax.axis_index(GROUP)]).astype(jnp.int32)
    rows = grad.shape[0]
    width = in_eigs.shape[0]
    anywhere = pl.BlockSpec(memory_space=pl.ANY)
    vmem = pl.BlockSpec(memory_space=pltpu.VMEM)
    return pl.pallas_call(
        precondition_kernel,
        out_shape=(
            jax.ShapeDtypeStruct((8, rows, width), jnp.bfloat16),
            jax.ShapeDtypeStruct((rows, width), jnp.float32),
        ),
        in_specs=[pl.BlockSpec(memory_space=pltpu.SMEM), anywhere, anywhere, vmem, vmem, vmem],
        out_specs=(vmem, vmem),
        scratch_shapes=[
            pltpu.VMEM((4, 8, 2, rows, width), jnp.bfloat16),
            pltpu.SemaphoreType.DMA((16,)),
        ],
        compiler_params=pltpu.CompilerParams(vmem_limit_bytes=58 << 20),
        cost_estimate=pl.CostEstimate(
            flops=4 * rows * 8 * width * width, bytes_accessed=24 * width * width, transcendentals=0
        ),
    )(place, own, other, grad, in_eigs[None, :], out_eigs[:, None])


def shards(activations, out_grads, counts, owners, rotated_grad, basis, input_eigs, output_eigs):
    slots, width = activations.shape
    owned_width = basis.shape[0]
    blocks_per = width // owned_width
    group_count = lax.axis_size("yl") * lax.axis_size("x")
    is_live = lax.broadcasted_iota(jnp.int32, (slots, 1), 0) < counts[0]
    kept_in, kept_out = (jnp.where(is_live, v, jnp.zeros_like(v)) for v in (activations, out_grads))
    column, kept_out = lax.optimization_barrier(
        (spread(jnp.concatenate([basis, kept_in]), "yh"), kept_out)
    )
    own = lax.all_gather(column[:, :owned_width], "z", axis=0)
    kept_in, kept_out = lax.optimization_barrier((column[:, owned_width:], spread(kept_out, "z")))
    kept_out = spread(kept_out.reshape(-1, width), "yh").reshape(-1, width)
    kept_in = lax.all_gather(kept_in.reshape(-1, width), "z", axis=0, tiled=True)
    kept = jnp.stack([kept_in, kept_out])
    both = jnp.concatenate([kept, shift(kept, "core", 1)], axis=1)
    samples = both.shape[1]
    owner_idx = owners[0]
    offset = owner_idx % blocks_per * owned_width
    owned = lax.dynamic_slice_in_dim(both, offset, owned_width, 2)
    pieces = owned.reshape(group_count, 2 * samples // group_count, owned_width)
    pieces = lax.all_to_all(pieces, GROUP, 0, 0, tiled=True)
    piece = lax.dynamic_index_in_dim(pieces, owner_idx // blocks_per, 0, keepdims=False)
    own, piece = lax.optimization_barrier((own, piece))
    owned = spread(piece, GROUP).reshape(2, samples, owned_width)
    contract_rows = (((0,), (0,)), ((), ()))
    cov_in, cov_out = (
        lax.dot_general(both[k], owned[k], contract_rows, preferred_element_type=jnp.float32)
        / jnp.float32(SAMPLED)
        for k in range(2)
    )

    other = shift(own, "core", 1)
    terms, own_term = precondition(own, other, rotated_grad, input_eigs, output_eigs)
    terms = lax.all_to_all(terms, GROUP, 0, 0, tiled=True)
    preconditioned = own_term + jnp.sum(terms.astype(jnp.float32), axis=0)
    return (cov_in, cov_out, preconditioned)


def solution(mesh):
    devices = mesh.devices.reshape(4, 8, 2, 2, 4)
    fine = Mesh(devices, DP + GROUP)
    placed = (
        P(DP, GROUP),
        P(DP, GROUP),
        P(DP),
        P(DP),
        P(DP, None),
        P(DP, GROUP),
        P(GROUP),
        P(DP),
    )
    return jax.shard_map(
        shards,
        mesh=fine,
        in_specs=placed,
        out_specs=(P(GROUP, DP), P(GROUP, DP), P(DP, GROUP)),
        check_vma=False,
    )
```

```python
import jax
import jax.numpy as jnp
from jax import lax
from jax.experimental import pallas as pl
from jax.experimental.pallas import tpu as pltpu
from jax.sharding import Mesh, PartitionSpec as P

DAMPING = 0.1
SAMPLED = 768
DP = ("yh", "z", "core")
GROUP = ("yl", "x")


def shift(value, axis, by):
    size = lax.axis_size(axis)
    return lax.ppermute(value, axis, [((i + by) % size, i) for i in range(size)])


def spread(block, axis):
    size = lax.axis_size(axis)
    return lax.all_to_all(jnp.broadcast_to(block[None], (size,) + block.shape), axis, 0, 0, tiled=True)


def precondition_kernel(place, own, other, grad, in_eigs, out_eigs, terms, kept, basis, sems):
    core, member = place[0], place[1]
    rows, width = in_eigs.shape[1], basis.shape[-1]
    steps = basis.shape[0] * 2
    copies = []
    for k in range(steps):
        y, zs = k // 2, pl.ds(k % 2 * 4, 4)
        copies.append(
            [
                pltpu.make_async_copy(src.at[zs, y], basis.at[y, zs, at], sems.at[2 * k + side])
                for side, (src, at) in enumerate(((own, core), (other, 1 - core)))
            ]
        )
    for pair in copies:
        for copy in pair:
            copy.start()

    def block(k):
        return basis[k // 2, k % 2 * 4 : k % 2 * 4 + 4].reshape(rows, width)

    projected = jnp.zeros((grad.shape[0], width), jnp.float32)
    for k in range(steps):
        for copy in copies[k]:
            copy.wait()
        projected += jnp.dot(
            grad[:, k * rows : (k + 1) * rows], block(k), preferred_element_type=jnp.float32
        )
    denominator = out_eigs[...] * in_eigs[...] + DAMPING
    scaled = (projected / denominator).astype(jnp.bfloat16)
    for k in range(steps):
        share = lax.dot_general(
            scaled, block(k), (((1,), (1,)), ((), ())), preferred_element_type=jnp.float32
        )

        @pl.when(member == k)
        def _():
            kept[...] = share

        terms[k] = jnp.where(member == k, 0.0, share).astype(terms.dtype)


def precondition(own, other, grad, in_eigs, out_eigs):
    place = jnp.stack([lax.axis_index("core"), lax.axis_index(GROUP)]).astype(jnp.int32)
    rows = grad.shape[0]
    width = in_eigs.shape[0]
    anywhere = pl.BlockSpec(memory_space=pl.ANY)
    vmem = pl.BlockSpec(memory_space=pltpu.VMEM)
    return pl.pallas_call(
        precondition_kernel,
        out_shape=(
            jax.ShapeDtypeStruct((8, rows, width), jnp.bfloat16),
            jax.ShapeDtypeStruct((rows, width), jnp.float32),
        ),
        in_specs=[pl.BlockSpec(memory_space=pltpu.SMEM), anywhere, anywhere, vmem, vmem, vmem],
        out_specs=(vmem, vmem),
        scratch_shapes=[
            pltpu.VMEM((4, 8, 2, rows, width), jnp.bfloat16),
            pltpu.SemaphoreType.DMA((16,)),
        ],
        compiler_params=pltpu.CompilerParams(vmem_limit_bytes=58 << 20),
        cost_estimate=pl.CostEstimate(
            flops=4 * rows * 8 * width * width, bytes_accessed=24 * width * width, transcendentals=0
        ),
    )(place, own, other, grad, in_eigs[None, :], out_eigs[:, None])


def shards(activations, out_grads, counts, owners, rotated_grad, basis, input_eigs, output_eigs):
    slots, width = activations.shape
    owned_width = basis.shape[0]
    blocks_per = width // owned_width
    group_count = lax.axis_size("yl") * lax.axis_size("x")
    is_live = lax.broadcasted_iota(jnp.int32, (slots, 1), 0) < counts[0]
    kept_in, kept_out = (jnp.where(is_live, v, jnp.zeros_like(v)) for v in (activations, out_grads))
    column, kept_out = lax.optimization_barrier(
        (spread(jnp.concatenate([basis, kept_in]), "yh"), kept_out)
    )
    own = lax.all_gather(column[:, :owned_width], "z", axis=0)
    kept_in, kept_out = lax.optimization_barrier((column[:, owned_width:], spread(kept_out, "z")))
    kept_out = spread(kept_out.reshape(-1, width), "yh").reshape(-1, width)
    kept_in = lax.all_gather(kept_in.reshape(-1, width), "z", axis=0, tiled=True)
    theirs = shift(jnp.stack([kept_in, kept_out]), "core", 1)
    samples = [(kept_in, theirs[0]), (kept_out, theirs[1])]
    owner_idx = owners[0]
    offset = owner_idx % blocks_per * owned_width
    owned = jnp.concatenate(
        [lax.dynamic_slice_in_dim(v, offset, owned_width, 1) for pair in samples for v in pair]
    )
    pieces = owned.reshape(group_count, -1, owned_width)
    arrived = lax.all_to_all(pieces, GROUP, 0, 0, tiled=True)
    piece = lax.dynamic_index_in_dim(arrived, owner_idx // blocks_per, 0, keepdims=False)
    own, piece = lax.optimization_barrier((own, piece))
    owned = spread(piece, GROUP).reshape(2, 2, -1, owned_width)
    contract_rows = (((0,), (0,)), ((), ()))
    cov_in, cov_out = (
        sum(
            lax.dot_general(v, part, contract_rows, preferred_element_type=jnp.float32)
            for v, part in zip(pair, parts)
        )
        / jnp.float32(SAMPLED)
        for pair, parts in zip(samples, owned)
    )

    other = shift(own, "core", 1)
    terms, own_term = precondition(own, other, rotated_grad, input_eigs, output_eigs)
    terms = lax.all_to_all(terms, GROUP, 0, 0, tiled=True)
    preconditioned = own_term + jnp.sum(terms.astype(jnp.float32), axis=0)
    return (cov_in, cov_out, preconditioned)


def solution(mesh):
    devices = mesh.devices.reshape(4, 8, 2, 2, 4)
    fine = Mesh(devices, DP + GROUP)
    placed = (
        P(DP, GROUP),
        P(DP, GROUP),
        P(DP),
        P(DP),
        P(DP, None),
        P(DP, GROUP),
        P(GROUP),
        P(DP),
    )
    return jax.shard_map(
        shards,
        mesh=fine,
        in_specs=placed,
        out_specs=(P(GROUP, DP), P(GROUP, DP), P(DP, GROUP)),
        check_vma=False,
    )
```

```python
import jax
import jax.numpy as jnp
from jax import lax
from jax.experimental import pallas as pl
from jax.experimental.pallas import tpu as pltpu
from jax.sharding import Mesh, PartitionSpec as P

DAMPING = 0.1
SAMPLED = 768
DP = ("yh", "z", "core")
GROUP = ("yl", "x")


def shift(value, axis, by):
    size = lax.axis_size(axis)
    return lax.ppermute(value, axis, [((i + by) % size, i) for i in range(size)])


def spread(block, axis):
    size = lax.axis_size(axis)
    return lax.all_to_all(jnp.broadcast_to(block[None], (size,) + block.shape), axis, 0, 0, tiled=True)


def precondition_kernel(place, own, other, grad, in_eigs, out_eigs, terms, kept, basis, sems):
    core, member = place[0], place[1]
    rows, width = in_eigs.shape[1], basis.shape[-1]
    steps = basis.shape[0] * 2
    copies = []
    for k in range(steps):
        y, zs = k // 2, pl.ds(k % 2 * 4, 4)
        copies.append(
            [
                pltpu.make_async_copy(src.at[zs, y], basis.at[y, zs, at], sems.at[2 * k + side])
                for side, (src, at) in enumerate(((own, core), (other, 1 - core)))
            ]
        )
    for pair in copies:
        for copy in pair:
            copy.start()

    def block(k):
        return basis[k // 2, k % 2 * 4 : k % 2 * 4 + 4].reshape(rows, width)

    projected = jnp.zeros((grad.shape[0], width), jnp.float32)
    for k in range(steps):
        for copy in copies[k]:
            copy.wait()
        projected += jnp.dot(
            grad[:, k * rows : (k + 1) * rows], block(k), preferred_element_type=jnp.float32
        )
    denominator = out_eigs[...] * in_eigs[...] + DAMPING
    scaled = (projected / denominator).astype(jnp.bfloat16)
    for k in range(steps):
        share = lax.dot_general(
            scaled, block(k), (((1,), (1,)), ((), ())), preferred_element_type=jnp.float32
        )

        @pl.when(member == k)
        def _():
            kept[...] = share

        terms[k] = jnp.where(member == k, 0.0, share).astype(terms.dtype)


def precondition(own, other, grad, in_eigs, out_eigs):
    place = jnp.stack([lax.axis_index("core"), lax.axis_index(GROUP)]).astype(jnp.int32)
    rows = grad.shape[0]
    width = in_eigs.shape[0]
    anywhere = pl.BlockSpec(memory_space=pl.ANY)
    vmem = pl.BlockSpec(memory_space=pltpu.VMEM)
    return pl.pallas_call(
        precondition_kernel,
        out_shape=(
            jax.ShapeDtypeStruct((8, rows, width), jnp.bfloat16),
            jax.ShapeDtypeStruct((rows, width), jnp.float32),
        ),
        in_specs=[pl.BlockSpec(memory_space=pltpu.SMEM), anywhere, anywhere, vmem, vmem, vmem],
        out_specs=(vmem, vmem),
        scratch_shapes=[
            pltpu.VMEM((4, 8, 2, rows, width), jnp.bfloat16),
            pltpu.SemaphoreType.DMA((16,)),
        ],
        compiler_params=pltpu.CompilerParams(vmem_limit_bytes=58 << 20),
        cost_estimate=pl.CostEstimate(
            flops=4 * rows * 8 * width * width, bytes_accessed=24 * width * width, transcendentals=0
        ),
    )(place, own, other, grad, in_eigs[None, :], out_eigs[:, None])


def shards(activations, out_grads, counts, owners, rotated_grad, basis, input_eigs, output_eigs):
    slots, width = activations.shape
    owned_width = basis.shape[0]
    blocks_per = width // owned_width
    group_count = lax.axis_size("yl") * lax.axis_size("x")
    is_live = lax.broadcasted_iota(jnp.int32, (slots, 1), 0) < counts[0]
    kept_in, kept_out = (jnp.where(is_live, v, jnp.zeros_like(v)) for v in (activations, out_grads))
    column, kept_out, partner = lax.optimization_barrier(
        (spread(jnp.concatenate([basis, kept_in]), "yh"), kept_out, shift(owners, "core", 1))
    )
    owner_pair = owners[0], partner[0]
    own = lax.all_gather(column[:, :owned_width], "z", axis=0)
    kept_in, kept_out = lax.optimization_barrier((column[:, owned_width:], spread(kept_out, "z")))
    kept_out = spread(kept_out.reshape(-1, width), "yh").reshape(-1, width)
    kept_in = lax.all_gather(kept_in.reshape(-1, width), "z", axis=0, tiled=True)
    samples = jnp.stack([kept_in, kept_out])
    pieces = []
    for idx in owner_pair:
        offset = idx % blocks_per * owned_width
        columns = [lax.dynamic_slice_in_dim(v, offset, owned_width, 1) for v in (kept_in, kept_out)]
        pieces.append(jnp.concatenate(columns).reshape(group_count, -1, owned_width))
    arrived = lax.all_to_all(jnp.concatenate(pieces, axis=1), GROUP, 0, 0, tiled=True)
    rows = pieces[0].shape[1]
    piece, for_other = (
        lax.dynamic_slice(arrived, (idx // blocks_per, k * rows, 0), (1, rows, owned_width))[0]
        for k, idx in enumerate(owner_pair)
    )
    own, piece, for_other = lax.optimization_barrier((own, piece, for_other))
    piece = jnp.concatenate([piece, shift(for_other, "core", 1)])
    owned = spread(piece, GROUP).reshape(group_count, 2, rows, owned_width)
    owned = jnp.moveaxis(owned, 1, 0).reshape(2, 2, -1, owned_width)
    theirs = shift(samples, "core", 1)
    contract_rows = (((0,), (0,)), ((), ()))
    cov_in, cov_out = (
        (
            lax.dot_general(mine, owned[0, k], contract_rows, preferred_element_type=jnp.float32)
            + lax.dot_general(theirs[k], owned[1, k], contract_rows, preferred_element_type=jnp.float32)
        )
        / jnp.float32(SAMPLED)
        for k, mine in enumerate((kept_in, kept_out))
    )

    other = shift(own, "core", 1)
    terms, own_term = precondition(own, other, rotated_grad, input_eigs, output_eigs)
    terms = lax.all_to_all(terms, GROUP, 0, 0, tiled=True)
    preconditioned = own_term + jnp.sum(terms.astype(jnp.float32), axis=0)
    return (cov_in, cov_out, preconditioned)


def solution(mesh):
    devices = mesh.devices.reshape(4, 8, 2, 2, 4)
    fine = Mesh(devices, DP + GROUP)
    placed = (
        P(DP, GROUP),
        P(DP, GROUP),
        P(DP),
        P(DP),
        P(DP, None),
        P(DP, GROUP),
        P(GROUP),
        P(DP),
    )
    return jax.shard_map(
        shards,
        mesh=fine,
        in_specs=placed,
        out_specs=(P(GROUP, DP), P(GROUP, DP), P(DP, GROUP)),
        check_vma=False,
    )
```

```python
import jax
import jax.numpy as jnp
from jax import lax
from jax.experimental import pallas as pl
from jax.experimental.pallas import tpu as pltpu
from jax.sharding import Mesh, PartitionSpec as P

DAMPING = 0.1
SAMPLED = 768
DP = ("yh", "z", "core")
GROUP = ("yl", "x")


def shift(value, axis, by):
    size = lax.axis_size(axis)
    return lax.ppermute(value, axis, [((i + by) % size, i) for i in range(size)])


def spread(block, axis):
    size = lax.axis_size(axis)
    return lax.all_to_all(jnp.broadcast_to(block[None], (size,) + block.shape), axis, 0, 0, tiled=True)


def precondition_kernel(place, own, other, grad, in_eigs, out_eigs, terms, kept, basis, sems):
    core, member = place[0], place[1]
    rows, width = in_eigs.shape[1], basis.shape[-1]
    steps = basis.shape[0] * 2
    copies = []
    for k in range(steps):
        y, zs = k // 2, pl.ds(k % 2 * 4, 4)
        copies.append(
            [
                pltpu.make_async_copy(src.at[zs, y], basis.at[y, zs, at], sems.at[2 * k + side])
                for side, (src, at) in enumerate(((own, core), (other, 1 - core)))
            ]
        )
    for pair in copies:
        for copy in pair:
            copy.start()

    def block(k):
        return basis[k // 2, k % 2 * 4 : k % 2 * 4 + 4].reshape(rows, width)

    projected = jnp.zeros((grad.shape[0], width), jnp.float32)
    for k in range(steps):
        for copy in copies[k]:
            copy.wait()
        projected += jnp.dot(
            grad[:, k * rows : (k + 1) * rows], block(k), preferred_element_type=jnp.float32
        )
    denominator = out_eigs[...] * in_eigs[...] + DAMPING
    scaled = (projected / denominator).astype(jnp.bfloat16)
    for k in range(steps):
        share = lax.dot_general(
            scaled, block(k), (((1,), (1,)), ((), ())), preferred_element_type=jnp.float32
        )

        @pl.when(member == k)
        def _():
            kept[...] = share

        terms[k] = jnp.where(member == k, 0.0, share).astype(terms.dtype)


def precondition(own, other, grad, in_eigs, out_eigs):
    place = jnp.stack([lax.axis_index("core"), lax.axis_index(GROUP)]).astype(jnp.int32)
    rows = grad.shape[0]
    width = in_eigs.shape[0]
    anywhere = pl.BlockSpec(memory_space=pl.ANY)
    vmem = pl.BlockSpec(memory_space=pltpu.VMEM)
    return pl.pallas_call(
        precondition_kernel,
        out_shape=(
            jax.ShapeDtypeStruct((8, rows, width), jnp.bfloat16),
            jax.ShapeDtypeStruct((rows, width), jnp.float32),
        ),
        in_specs=[pl.BlockSpec(memory_space=pltpu.SMEM), anywhere, anywhere, vmem, vmem, vmem],
        out_specs=(vmem, vmem),
        scratch_shapes=[
            pltpu.VMEM((4, 8, 2, rows, width), jnp.bfloat16),
            pltpu.SemaphoreType.DMA((16,)),
        ],
        compiler_params=pltpu.CompilerParams(vmem_limit_bytes=58 << 20),
        cost_estimate=pl.CostEstimate(
            flops=4 * rows * 8 * width * width, bytes_accessed=24 * width * width, transcendentals=0
        ),
    )(place, own, other, grad, in_eigs[None, :], out_eigs[:, None])


def shards(activations, out_grads, counts, owners, rotated_grad, basis, input_eigs, output_eigs):
    slots, width = activations.shape
    owned_width = basis.shape[0]
    blocks_per = width // owned_width
    group_count = lax.axis_size("yl") * lax.axis_size("x")
    is_live = lax.broadcasted_iota(jnp.int32, (slots, 1), 0) < counts[0]
    kept_in, kept_out = (jnp.where(is_live, v, jnp.zeros_like(v)) for v in (activations, out_grads))
    column, kept_out, partner = lax.optimization_barrier(
        (spread(jnp.concatenate([basis, kept_in]), "yh"), kept_out, shift(owners, "core", 1))
    )
    owner_pair = owners[0], partner[0]
    own = lax.all_gather(column[:, :owned_width], "z", axis=0)
    kept_in, kept_out = lax.optimization_barrier((column[:, owned_width:], spread(kept_out, "z")))
    kept_out = spread(kept_out.reshape(-1, width), "yh").reshape(-1, width)
    kept_in = lax.all_gather(kept_in.reshape(-1, width), "z", axis=0, tiled=True)
    pieces = []
    for idx in owner_pair:
        offset = idx % blocks_per * owned_width
        columns = [lax.dynamic_slice_in_dim(v, offset, owned_width, 1) for v in (kept_in, kept_out)]
        pieces.append(jnp.concatenate(columns).reshape(group_count, -1, owned_width))
    arrived = lax.all_to_all(jnp.concatenate(pieces, axis=1), GROUP, 0, 0, tiled=True)
    rows = pieces[0].shape[1]
    piece, for_other = (
        lax.dynamic_slice(arrived, (idx // blocks_per, k * rows, 0), (1, rows, owned_width))[0]
        for k, idx in enumerate(owner_pair)
    )
    theirs = shift(jnp.stack([kept_in, kept_out]), "core", 1)
    own, piece, for_other, theirs = lax.optimization_barrier((own, piece, for_other, theirs))
    core = lax.axis_index("core")
    shares = jnp.stack([jnp.where(core == k, piece, for_other) for k in range(2)])
    shares = jnp.broadcast_to(shares[:, None], (2, group_count) + piece.shape)
    owned = lax.all_to_all(
        shares.reshape((-1,) + piece.shape), ("core",) + GROUP, 0, 0, tiled=True
    ).reshape(2, 2, -1, owned_width)
    owned_mine, owned_theirs = (
        lax.dynamic_index_in_dim(owned, k, 0, keepdims=False) for k in (core, 1 - core)
    )
    contract_rows = (((0,), (0,)), ((), ()))
    cov_in, cov_out = (
        (
            lax.dot_general(mine, owned_mine[k], contract_rows, preferred_element_type=jnp.float32)
            + lax.dot_general(theirs[k], owned_theirs[k], contract_rows, preferred_element_type=jnp.float32)
        )
        / jnp.float32(SAMPLED)
        for k, mine in enumerate((kept_in, kept_out))
    )

    other = shift(own, "core", 1)
    terms, own_term = precondition(own, other, rotated_grad, input_eigs, output_eigs)
    terms = lax.all_to_all(terms, GROUP, 0, 0, tiled=True)
    preconditioned = own_term + jnp.sum(terms.astype(jnp.float32), axis=0)
    return (cov_in, cov_out, preconditioned)


def solution(mesh):
    devices = mesh.devices.reshape(4, 8, 2, 2, 4)
    fine = Mesh(devices, DP + GROUP)
    placed = (
        P(DP, GROUP),
        P(DP, GROUP),
        P(DP),
        P(DP),
        P(DP, None),
        P(DP, GROUP),
        P(GROUP),
        P(DP),
    )
    return jax.shard_map(
        shards,
        mesh=fine,
        in_specs=placed,
        out_specs=(P(GROUP, DP), P(GROUP, DP), P(DP, GROUP)),
        check_vma=False,
    )
```

```python
import jax
import jax.numpy as jnp
from jax import lax
from jax.experimental import pallas as pl
from jax.experimental.pallas import tpu as pltpu
from jax.sharding import Mesh, PartitionSpec as P

DAMPING = 0.1
SAMPLED = 768
DP = ("yh", "z", "core")
GROUP = ("yl", "x")


def shift(value, axis, by):
    size = lax.axis_size(axis)
    return lax.ppermute(value, axis, [((i + by) % size, i) for i in range(size)])


def spread(block, axis):
    size = lax.axis_size(axis)
    return lax.all_to_all(jnp.broadcast_to(block[None], (size,) + block.shape), axis, 0, 0, tiled=True)


def precondition_kernel(place, own, other, grad, in_eigs, out_eigs, terms, kept, basis, sems):
    core, member = place[0], place[1]
    rows, width = in_eigs.shape[1], basis.shape[-1]
    steps = basis.shape[0] * 2
    copies = []
    for k in range(steps):
        y, zs = k // 2, pl.ds(k % 2 * 4, 4)
        copies.append(
            [
                pltpu.make_async_copy(src.at[zs, y], basis.at[y, zs, at], sems.at[2 * k + side])
                for side, (src, at) in enumerate(((own, core), (other, 1 - core)))
            ]
        )
    for pair in copies:
        for copy in pair:
            copy.start()

    def block(k):
        return basis[k // 2, k % 2 * 4 : k % 2 * 4 + 4].reshape(rows, width)

    projected = jnp.zeros((grad.shape[0], width), jnp.float32)
    for k in range(steps):
        for copy in copies[k]:
            copy.wait()
        projected += jnp.dot(
            grad[:, k * rows : (k + 1) * rows], block(k), preferred_element_type=jnp.float32
        )
    denominator = out_eigs[...] * in_eigs[...] + DAMPING
    scaled = (projected / denominator).astype(jnp.bfloat16)
    for k in range(steps):
        share = lax.dot_general(
            scaled, block(k), (((1,), (1,)), ((), ())), preferred_element_type=jnp.float32
        )

        @pl.when(member == k)
        def _():
            kept[...] = share

        terms[k] = jnp.where(member == k, 0.0, share).astype(terms.dtype)


def precondition(own, other, grad, in_eigs, out_eigs):
    place = jnp.stack([lax.axis_index("core"), lax.axis_index(GROUP)]).astype(jnp.int32)
    rows = grad.shape[0]
    width = in_eigs.shape[0]
    anywhere = pl.BlockSpec(memory_space=pl.ANY)
    vmem = pl.BlockSpec(memory_space=pltpu.VMEM)
    return pl.pallas_call(
        precondition_kernel,
        out_shape=(
            jax.ShapeDtypeStruct((8, rows, width), jnp.bfloat16),
            jax.ShapeDtypeStruct((rows, width), jnp.float32),
        ),
        in_specs=[pl.BlockSpec(memory_space=pltpu.SMEM), anywhere, anywhere, vmem, vmem, vmem],
        out_specs=(vmem, vmem),
        scratch_shapes=[
            pltpu.VMEM((4, 8, 2, rows, width), jnp.bfloat16),
            pltpu.SemaphoreType.DMA((16,)),
        ],
        compiler_params=pltpu.CompilerParams(vmem_limit_bytes=20 << 20),
        cost_estimate=pl.CostEstimate(
            flops=4 * rows * 8 * width * width, bytes_accessed=24 * width * width, transcendentals=0
        ),
    )(place, own, other, grad, in_eigs[None, :], out_eigs[:, None])


def shards(activations, out_grads, counts, owners, rotated_grad, basis, input_eigs, output_eigs):
    slots, width = activations.shape
    owned_width = basis.shape[0]
    blocks_per = width // owned_width
    group_count = lax.axis_size("yl") * lax.axis_size("x")
    is_live = lax.broadcasted_iota(jnp.int32, (slots, 1), 0) < counts[0]
    kept_in, kept_out = (jnp.where(is_live, v, jnp.zeros_like(v)) for v in (activations, out_grads))
    column, kept_out, partner = lax.optimization_barrier(
        (spread(jnp.concatenate([basis, kept_in]), "yh"), kept_out, shift(owners, "core", 1))
    )
    owner_pair = owners[0], partner[0]
    own = lax.all_gather(column[:, :owned_width], "z", axis=0)
    kept_in, kept_out = lax.optimization_barrier((column[:, owned_width:], spread(kept_out, "z")))
    kept_out = spread(kept_out.reshape(-1, width), "yh").reshape(-1, width)
    kept_in = lax.all_gather(kept_in.reshape(-1, width), "z", axis=0, tiled=True)
    pieces = []
    for idx in owner_pair:
        offset = idx % blocks_per * owned_width
        columns = [lax.dynamic_slice_in_dim(v, offset, owned_width, 1) for v in (kept_in, kept_out)]
        pieces.append(jnp.concatenate(columns).reshape(group_count, -1, owned_width))
    arrived = lax.all_to_all(jnp.concatenate(pieces, axis=1), GROUP, 0, 0, tiled=True)
    rows = pieces[0].shape[1]
    piece, for_other = (
        lax.dynamic_slice(arrived, (idx // blocks_per, k * rows, 0), (1, rows, owned_width))[0]
        for k, idx in enumerate(owner_pair)
    )
    theirs = shift(jnp.stack([kept_in, kept_out]), "core", 1)
    own, piece, for_other, theirs = lax.optimization_barrier((own, piece, for_other, theirs))
    core = lax.axis_index("core")
    shares = jnp.stack([jnp.where(core == k, piece, for_other) for k in range(2)])
    shares = jnp.broadcast_to(shares[:, None], (2, group_count) + piece.shape)
    owned = lax.all_to_all(
        shares.reshape((-1,) + piece.shape), ("core",) + GROUP, 0, 0, tiled=True
    ).reshape(2, 2, -1, owned_width)
    owned_mine, owned_theirs = (
        lax.dynamic_index_in_dim(owned, k, 0, keepdims=False) for k in (core, 1 - core)
    )
    contract_rows = (((0,), (0,)), ((), ()))
    cov_in, cov_out = (
        (
            lax.dot_general(mine, owned_mine[k], contract_rows, preferred_element_type=jnp.float32)
            + lax.dot_general(theirs[k], owned_theirs[k], contract_rows, preferred_element_type=jnp.float32)
        )
        / jnp.float32(SAMPLED)
        for k, mine in enumerate((kept_in, kept_out))
    )

    other = shift(own, "core", 1)
    terms, own_term = precondition(own, other, rotated_grad, input_eigs, output_eigs)
    terms = lax.all_to_all(terms, GROUP, 0, 0, tiled=True)
    preconditioned = own_term + jnp.sum(terms.astype(jnp.float32), axis=0)
    return (cov_in, cov_out, preconditioned)


def solution(mesh):
    devices = mesh.devices.reshape(4, 8, 2, 2, 4)
    fine = Mesh(devices, DP + GROUP)
    placed = (
        P(DP, GROUP),
        P(DP, GROUP),
        P(DP),
        P(DP),
        P(DP, None),
        P(DP, GROUP),
        P(GROUP),
        P(DP),
    )
    return jax.shard_map(
        shards,
        mesh=fine,
        in_specs=placed,
        out_specs=(P(GROUP, DP), P(GROUP, DP), P(DP, GROUP)),
        check_vma=False,
    )
```

```python
import jax
import jax.numpy as jnp
from jax import lax
from jax.experimental import pallas as pl
from jax.experimental.pallas import tpu as pltpu
from jax.sharding import Mesh, PartitionSpec as P

DAMPING = 0.1
SAMPLED = 768
DP = ("yh", "z", "core")
GROUP = ("yl", "x")


def shift(value, axis, by):
    size = lax.axis_size(axis)
    return lax.ppermute(value, axis, [((i + by) % size, i) for i in range(size)])


def spread(block, axis):
    size = lax.axis_size(axis)
    return lax.all_to_all(jnp.broadcast_to(block[None], (size,) + block.shape), axis, 0, 0, tiled=True)


def precondition_kernel(place, own, other, grad, in_eigs, out_eigs, terms, kept, basis, sems):
    core, member = place[0], place[1]
    rows, width = in_eigs.shape[1], basis.shape[-1]
    steps = basis.shape[0] * 2
    copies = []
    for k in range(steps):
        y, zs = k // 2, pl.ds(k % 2 * 4, 4)
        copies.append(
            [
                pltpu.make_async_copy(src.at[zs, y], basis.at[y, zs, at], sems.at[2 * k + side])
                for side, (src, at) in enumerate(((own, core), (other, 1 - core)))
            ]
        )
    for pair in copies:
        for copy in pair:
            copy.start()

    def block(k):
        return basis[k // 2, k % 2 * 4 : k % 2 * 4 + 4].reshape(rows, width)

    projected = jnp.zeros((grad.shape[0], width), jnp.float32)
    for k in range(steps):
        for copy in copies[k]:
            copy.wait()
        projected += jnp.dot(
            grad[:, k * rows : (k + 1) * rows], block(k), preferred_element_type=jnp.float32
        )
    denominator = out_eigs[...] * in_eigs[...] + DAMPING
    scaled = (projected / denominator).astype(jnp.bfloat16)
    for k in range(steps):
        share = lax.dot_general(
            scaled, block(k), (((1,), (1,)), ((), ())), preferred_element_type=jnp.float32
        )

        @pl.when(member == k)
        def _():
            kept[...] = share

        terms[k] = jnp.where(member == k, 0.0, share).astype(terms.dtype)


def precondition(own, other, grad, in_eigs, out_eigs):
    place = jnp.stack([lax.axis_index("core"), lax.axis_index(GROUP)]).astype(jnp.int32)
    rows = grad.shape[0]
    width = in_eigs.shape[0]
    hbm = pl.BlockSpec(memory_space=pltpu.HBM)
    vmem = pl.BlockSpec(memory_space=pltpu.VMEM)
    return pl.pallas_call(
        precondition_kernel,
        out_shape=(
            jax.ShapeDtypeStruct((8, rows, width), jnp.bfloat16),
            jax.ShapeDtypeStruct((rows, width), jnp.float32),
        ),
        in_specs=[pl.BlockSpec(memory_space=pltpu.SMEM), hbm, hbm, vmem, vmem, vmem],
        out_specs=(vmem, vmem),
        scratch_shapes=[
            pltpu.VMEM((4, 8, 2, rows, width), jnp.bfloat16),
            pltpu.SemaphoreType.DMA((16,)),
        ],
        compiler_params=pltpu.CompilerParams(vmem_limit_bytes=50 << 20),
        cost_estimate=pl.CostEstimate(
            flops=4 * rows * 8 * width * width, bytes_accessed=24 * width * width, transcendentals=0
        ),
    )(place, own, other, grad, in_eigs[None, :], out_eigs[:, None])


def shards(activations, out_grads, counts, owners, rotated_grad, basis, input_eigs, output_eigs):
    slots, width = activations.shape
    owned_width = basis.shape[0]
    blocks_per = width // owned_width
    group_count = lax.axis_size("yl") * lax.axis_size("x")
    is_live = lax.broadcasted_iota(jnp.int32, (slots, 1), 0) < counts[0]
    kept_in, kept_out = (jnp.where(is_live, v, jnp.zeros_like(v)) for v in (activations, out_grads))
    owner_pair = [
        (lax.rem(idx, blocks_per) * owned_width, lax.div(idx, blocks_per))
        for idx in (owners[0], shift(owners, "core", 1)[0])
    ]
    column, kept_out, owner_pair = lax.optimization_barrier(
        (spread(jnp.concatenate([basis, kept_in]), "yh"), kept_out, owner_pair)
    )
    own = lax.all_gather(column[:, :owned_width], "z", axis=0)
    kept_in, kept_out = lax.optimization_barrier((column[:, owned_width:], spread(kept_out, "z")))
    kept_out = spread(kept_out.reshape(-1, width), "yh").reshape(-1, width)
    kept_in = lax.all_gather(kept_in.reshape(-1, width), "z", axis=0, tiled=True)
    pieces = []
    for offset, _ in owner_pair:
        columns = [lax.dynamic_slice_in_dim(v, offset, owned_width, 1) for v in (kept_in, kept_out)]
        pieces.append(jnp.concatenate(columns).reshape(group_count, -1, owned_width))
    arrived = lax.all_to_all(jnp.concatenate(pieces, axis=1), GROUP, 0, 0, tiled=True)
    rows = pieces[0].shape[1]
    piece, for_other = (
        lax.dynamic_slice(arrived, (root, k * rows, 0), (1, rows, owned_width))[0]
        for k, (_, root) in enumerate(owner_pair)
    )
    theirs = shift(jnp.stack([kept_in, kept_out]), "core", 1)
    own, piece, for_other, theirs = lax.optimization_barrier((own, piece, for_other, theirs))
    core = lax.axis_index("core")
    shares = jnp.stack([jnp.where(core == k, piece, for_other) for k in range(2)])
    shares = jnp.broadcast_to(shares[:, None], (2, group_count) + piece.shape)
    owned = lax.all_to_all(
        shares.reshape((-1,) + piece.shape), ("core",) + GROUP, 0, 0, tiled=True
    ).reshape(2, 2, -1, owned_width)
    owned_mine, owned_theirs = (
        lax.dynamic_index_in_dim(owned, k, 0, keepdims=False) for k in (core, 1 - core)
    )
    contract_rows = (((0,), (0,)), ((), ()))
    cov_in, cov_out = (
        (
            lax.dot_general(mine, owned_mine[k], contract_rows, preferred_element_type=jnp.float32)
            + lax.dot_general(theirs[k], owned_theirs[k], contract_rows, preferred_element_type=jnp.float32)
        )
        / jnp.float32(SAMPLED)
        for k, mine in enumerate((kept_in, kept_out))
    )

    other = shift(own, "core", 1)
    terms, own_term = precondition(own, other, rotated_grad, input_eigs, output_eigs)
    terms = lax.all_to_all(terms, GROUP, 0, 0, tiled=True)
    preconditioned = own_term + jnp.sum(terms.astype(jnp.float32), axis=0)
    return (cov_in, cov_out, preconditioned)


def solution(mesh):
    devices = mesh.devices.reshape(4, 8, 2, 2, 4)
    fine = Mesh(devices, DP + GROUP)
    placed = (
        P(DP, GROUP),
        P(DP, GROUP),
        P(DP),
        P(DP),
        P(DP, None),
        P(DP, GROUP),
        P(GROUP),
        P(DP),
    )
    return jax.shard_map(
        shards,
        mesh=fine,
        in_specs=placed,
        out_specs=(P(GROUP, DP), P(GROUP, DP), P(DP, GROUP)),
        check_vma=False,
    )
```

```python
import jax
import jax.numpy as jnp
from jax import lax
from jax.experimental import pallas as pl
from jax.experimental.pallas import tpu as pltpu
from jax.sharding import Mesh, PartitionSpec as P

DAMPING = 0.1
SAMPLED = 768
DP = ("yh", "z", "core")
GROUP = ("yl", "x")


def shift(value, axis, by):
    size = lax.axis_size(axis)
    return lax.ppermute(value, axis, [((i + by) % size, i) for i in range(size)])


def spread(block, axis):
    size = lax.axis_size(axis)
    return lax.all_to_all(jnp.broadcast_to(block[None], (size,) + block.shape), axis, 0, 0, tiled=True)


def precondition_kernel(place, own, other, grad, in_eigs, out_eigs, terms, kept, basis, sems):
    core, member = place[0], place[1]
    rows, width = in_eigs.shape[1], basis.shape[-1]
    steps = basis.shape[0] * 2
    copies = []
    for k in range(steps):
        y, zs = k // 2, pl.ds(k % 2 * 4, 4)
        copies.append(
            [
                pltpu.make_async_copy(src.at[zs, y], basis.at[y, zs, at], sems.at[2 * k + side])
                for side, (src, at) in enumerate(((own, core), (other, 1 - core)))
            ]
        )
    for pair in copies:
        for copy in pair:
            copy.start()

    def block(k):
        return basis[k // 2, k % 2 * 4 : k % 2 * 4 + 4].reshape(rows, width)

    projected = jnp.zeros((grad.shape[0], width), jnp.float32)
    for k in range(steps):
        for copy in copies[k]:
            copy.wait()
        projected += jnp.dot(
            grad[:, k * rows : (k + 1) * rows], block(k), preferred_element_type=jnp.float32
        )
    denominator = out_eigs[...] * in_eigs[...] + DAMPING
    scaled = (projected / denominator).astype(jnp.bfloat16)
    for k in range(steps):
        share = lax.dot_general(
            scaled, block(k), (((1,), (1,)), ((), ())), preferred_element_type=jnp.float32
        )

        @pl.when(member == k)
        def _():
            kept[...] = share

        terms[k] = jnp.where(member == k, 0.0, share).astype(terms.dtype)


def precondition(own, other, grad, in_eigs, out_eigs):
    place = jnp.stack([lax.axis_index("core"), lax.axis_index(GROUP)]).astype(jnp.int32)
    rows = grad.shape[0]
    width = in_eigs.shape[0]
    hbm = pl.BlockSpec(memory_space=pltpu.HBM)
    vmem = pl.BlockSpec(memory_space=pltpu.VMEM)
    return pl.pallas_call(
        precondition_kernel,
        out_shape=(
            jax.ShapeDtypeStruct((8, rows, width), jnp.bfloat16),
            jax.ShapeDtypeStruct((rows, width), jnp.float32),
        ),
        in_specs=[pl.BlockSpec(memory_space=pltpu.SMEM), hbm, hbm, vmem, vmem, vmem],
        out_specs=(vmem, vmem),
        scratch_shapes=[
            pltpu.VMEM((4, 8, 2, rows, width), jnp.bfloat16),
            pltpu.SemaphoreType.DMA((16,)),
        ],
        compiler_params=pltpu.CompilerParams(vmem_limit_bytes=50 << 20),
        cost_estimate=pl.CostEstimate(
            flops=4 * rows * 8 * width * width, bytes_accessed=24 * width * width, transcendentals=0
        ),
    )(place, own, other, grad, in_eigs[None, :], out_eigs[:, None])


def shards(activations, out_grads, counts, owners, rotated_grad, basis, input_eigs, output_eigs):
    slots, width = activations.shape
    owned_width = basis.shape[0]
    blocks_per = width // owned_width
    group_count = lax.axis_size("yl") * lax.axis_size("x")
    is_live = lax.broadcasted_iota(jnp.int32, (slots, 1), 0) < counts[0]
    kept_in, kept_out = (jnp.where(is_live, v, jnp.zeros_like(v)) for v in (activations, out_grads))
    owner_pair = [
        (lax.rem(idx, blocks_per) * owned_width, lax.div(idx, blocks_per))
        for idx in (owners[0], shift(owners, "core", 1)[0])
    ]
    column, kept_out, owner_pair = lax.optimization_barrier(
        (spread(jnp.concatenate([basis, kept_in]), "yh"), kept_out, owner_pair)
    )
    own = lax.all_gather(column[:, :owned_width], "z", axis=0)
    kept_in, kept_out = lax.optimization_barrier((column[:, owned_width:], spread(kept_out, "z")))
    kept_out = spread(kept_out.reshape(-1, width), "yh").reshape(-1, width)
    kept_in = lax.all_gather(kept_in.reshape(-1, width), "z", axis=0, tiled=True)
    pieces = []
    for offset, _ in owner_pair:
        columns = [lax.dynamic_slice_in_dim(v, offset, owned_width, 1) for v in (kept_in, kept_out)]
        pieces.append(jnp.concatenate(columns).reshape(group_count, -1, owned_width))
    arrived = lax.all_to_all(jnp.concatenate(pieces, axis=1), GROUP, 0, 0, tiled=True)
    rows = pieces[0].shape[1]
    piece, for_other = (
        lax.dynamic_slice(arrived, (root, k * rows, 0), (1, rows, owned_width))[0]
        for k, (_, root) in enumerate(owner_pair)
    )
    own, piece, for_other, samples = lax.optimization_barrier(
        (own, piece, for_other, (kept_in, kept_out))
    )
    theirs = shift(jnp.stack(samples), "core", 1)
    core = lax.axis_index("core")
    shares = jnp.stack([jnp.where(core == k, piece, for_other) for k in range(2)])
    shares = jnp.broadcast_to(shares[:, None], (2, group_count) + piece.shape)
    owned = lax.all_to_all(
        shares.reshape((-1,) + piece.shape), ("core",) + GROUP, 0, 0, tiled=True
    ).reshape(2, 2, -1, owned_width)
    owned_mine, owned_theirs = (
        lax.dynamic_index_in_dim(owned, k, 0, keepdims=False) for k in (core, 1 - core)
    )
    contract_rows = (((0,), (0,)), ((), ()))
    cov_in, cov_out = (
        (
            lax.dot_general(mine, owned_mine[k], contract_rows, preferred_element_type=jnp.float32)
            + lax.dot_general(theirs[k], owned_theirs[k], contract_rows, preferred_element_type=jnp.float32)
        )
        / jnp.float32(SAMPLED)
        for k, mine in enumerate((kept_in, kept_out))
    )

    other = shift(own, "core", 1)
    terms, own_term = precondition(own, other, rotated_grad, input_eigs, output_eigs)
    terms = lax.all_to_all(terms, GROUP, 0, 0, tiled=True)
    preconditioned = own_term + jnp.sum(terms.astype(jnp.float32), axis=0)
    return (cov_in, cov_out, preconditioned)


def solution(mesh):
    devices = mesh.devices.reshape(4, 8, 2, 2, 4)
    fine = Mesh(devices, DP + GROUP)
    placed = (
        P(DP, GROUP),
        P(DP, GROUP),
        P(DP),
        P(DP),
        P(DP, None),
        P(DP, GROUP),
        P(GROUP),
        P(DP),
    )
    return jax.shard_map(
        shards,
        mesh=fine,
        in_specs=placed,
        out_specs=(P(GROUP, DP), P(GROUP, DP), P(DP, GROUP)),
        check_vma=False,
    )
```

```python
import jax
import jax.numpy as jnp
from jax import lax
from jax.experimental import pallas as pl
from jax.experimental.pallas import tpu as pltpu
from jax.sharding import Mesh, PartitionSpec as P

DAMPING = 0.1
SAMPLED = 768
DP = ("yh", "z", "core")
GROUP = ("yl", "x")


def shift(value, axis, by):
    size = lax.axis_size(axis)
    return lax.ppermute(value, axis, [((i + by) % size, i) for i in range(size)])


def spread(block, axis):
    size = lax.axis_size(axis)
    return lax.all_to_all(jnp.broadcast_to(block[None], (size,) + block.shape), axis, 0, 0, tiled=True)


def precondition_kernel(place, own, other, grad, in_eigs, out_eigs, terms, kept, basis, sems):
    core, member = place[0], place[1]
    rows, width = in_eigs.shape[1], basis.shape[-1]
    steps = basis.shape[0] * 2
    copies = []
    for k in range(steps):
        y, zs = k // 2, pl.ds(k % 2 * 4, 4)
        copies.append(
            [
                pltpu.make_async_copy(src.at[zs, y], basis.at[y, zs, at], sems.at[2 * k + side])
                for side, (src, at) in enumerate(((own, core), (other, 1 - core)))
            ]
        )
    for pair in copies:
        for copy in pair:
            copy.start()

    def block(k):
        return basis[k // 2, k % 2 * 4 : k % 2 * 4 + 4].reshape(rows, width)

    projected = jnp.zeros((grad.shape[0], width), jnp.float32)
    for k in range(steps):
        for copy in copies[k]:
            copy.wait()
        projected += jnp.dot(
            grad[:, k * rows : (k + 1) * rows], block(k), preferred_element_type=jnp.float32
        )
    denominator = out_eigs[...] * in_eigs[...] + DAMPING
    scaled = (projected / denominator).astype(jnp.bfloat16)
    for k in range(steps):
        share = lax.dot_general(
            scaled, block(k), (((1,), (1,)), ((), ())), preferred_element_type=jnp.float32
        )

        @pl.when(member == k)
        def _():
            kept[...] = share

        terms[k] = jnp.where(member == k, 0.0, share).astype(terms.dtype)


def precondition(own, other, grad, in_eigs, out_eigs):
    place = jnp.stack([lax.axis_index("core"), lax.axis_index(GROUP)]).astype(jnp.int32)
    rows = grad.shape[0]
    width = in_eigs.shape[0]
    hbm = pl.BlockSpec(memory_space=pltpu.HBM)
    vmem = pl.BlockSpec(memory_space=pltpu.VMEM)
    return pl.pallas_call(
        precondition_kernel,
        out_shape=(
            jax.ShapeDtypeStruct((8, rows, width), jnp.bfloat16),
            jax.ShapeDtypeStruct((rows, width), jnp.float32),
        ),
        in_specs=[pl.BlockSpec(memory_space=pltpu.SMEM), hbm, hbm, vmem, vmem, vmem],
        out_specs=(vmem, vmem),
        scratch_shapes=[
            pltpu.VMEM((4, 8, 2, rows, width), jnp.bfloat16),
            pltpu.SemaphoreType.DMA((16,)),
        ],
        compiler_params=pltpu.CompilerParams(vmem_limit_bytes=50 << 20),
        cost_estimate=pl.CostEstimate(
            flops=4 * rows * 8 * width * width, bytes_accessed=24 * width * width, transcendentals=0
        ),
    )(place, own, other, grad, in_eigs[None, :], out_eigs[:, None])


def shards(activations, out_grads, counts, owners, rotated_grad, basis, input_eigs, output_eigs):
    slots, width = activations.shape
    owned_width = basis.shape[0]
    blocks_per = width // owned_width
    group_count = lax.axis_size("yl") * lax.axis_size("x")
    is_live = lax.broadcasted_iota(jnp.int32, (slots, 1), 0) < counts[0]
    kept_out = jnp.where(is_live, out_grads, jnp.zeros_like(out_grads))
    joined = jnp.concatenate([basis, activations])
    row = lax.broadcasted_iota(jnp.int32, (joined.shape[0], 1), 0)
    joined = jnp.where(row < owned_width + counts[0], joined, jnp.zeros_like(joined))
    owner_pair = [
        (lax.rem(idx, blocks_per) * owned_width, lax.div(idx, blocks_per))
        for idx in (owners[0], shift(owners, "core", 1)[0])
    ]
    column, kept_out, owner_pair = lax.optimization_barrier(
        (spread(joined, "yh"), kept_out, owner_pair)
    )
    own = lax.all_gather(column[:, :owned_width], "z", axis=0)
    kept_in, kept_out = lax.optimization_barrier((column[:, owned_width:], spread(kept_out, "z")))
    kept_out = spread(kept_out.reshape(-1, width), "yh").reshape(-1, width)
    kept_in = lax.all_gather(kept_in.reshape(-1, width), "z", axis=0, tiled=True)
    pieces = []
    for offset, _ in owner_pair:
        columns = [lax.dynamic_slice_in_dim(v, offset, owned_width, 1) for v in (kept_in, kept_out)]
        pieces.append(jnp.concatenate(columns).reshape(group_count, -1, owned_width))
    arrived = lax.all_to_all(jnp.concatenate(pieces, axis=1), GROUP, 0, 0, tiled=True)
    rows = pieces[0].shape[1]
    piece, for_other = (
        lax.dynamic_slice(arrived, (root, k * rows, 0), (1, rows, owned_width))[0]
        for k, (_, root) in enumerate(owner_pair)
    )
    theirs = shift(jnp.stack([kept_in, kept_out]), "core", 1)
    own, piece, for_other, theirs = lax.optimization_barrier((own, piece, for_other, theirs))
    core = lax.axis_index("core")
    shares = jnp.stack([jnp.where(core == k, piece, for_other) for k in range(2)])
    shares = jnp.broadcast_to(shares[:, None], (2, group_count) + piece.shape)
    owned = lax.all_to_all(
        shares.reshape((-1,) + piece.shape), ("core",) + GROUP, 0, 0, tiled=True
    ).reshape(2, 2, -1, owned_width)
    owned_mine, owned_theirs = (
        lax.dynamic_index_in_dim(owned, k, 0, keepdims=False) for k in (core, 1 - core)
    )
    contract_rows = (((0,), (0,)), ((), ()))
    cov_in, cov_out = (
        (
            lax.dot_general(mine, owned_mine[k], contract_rows, preferred_element_type=jnp.float32)
            + lax.dot_general(theirs[k], owned_theirs[k], contract_rows, preferred_element_type=jnp.float32)
        )
        / jnp.float32(SAMPLED)
        for k, mine in enumerate((kept_in, kept_out))
    )

    other = shift(own, "core", 1)
    terms, own_term = precondition(own, other, rotated_grad, input_eigs, output_eigs)
    terms = lax.all_to_all(terms, GROUP, 0, 0, tiled=True)
    preconditioned = own_term + jnp.sum(terms.astype(jnp.float32), axis=0)
    return (cov_in, cov_out, preconditioned)


def solution(mesh):
    devices = mesh.devices.reshape(4, 8, 2, 2, 4)
    fine = Mesh(devices, DP + GROUP)
    placed = (
        P(DP, GROUP),
        P(DP, GROUP),
        P(DP),
        P(DP),
        P(DP, None),
        P(DP, GROUP),
        P(GROUP),
        P(DP),
    )
    return jax.shard_map(
        shards,
        mesh=fine,
        in_specs=placed,
        out_specs=(P(GROUP, DP), P(GROUP, DP), P(DP, GROUP)),
        check_vma=False,
    )
```

```python
import jax
import jax.numpy as jnp
from jax import lax
from jax.experimental import pallas as pl
from jax.experimental.pallas import tpu as pltpu
from jax.sharding import Mesh, PartitionSpec as P

DAMPING = 0.1
SAMPLED = 768
DP = ("yh", "z", "core")
GROUP = ("yl", "x")


def shift(value, axis, by):
    size = lax.axis_size(axis)
    return lax.ppermute(value, axis, [((i + by) % size, i) for i in range(size)])


def spread(block, axis):
    size = lax.axis_size(axis)
    return lax.all_to_all(jnp.broadcast_to(block[None], (size,) + block.shape), axis, 0, 0, tiled=True)


def precondition_kernel(place, own, other, grad, in_eigs, out_eigs, terms, kept, basis, staged, sems):
    core, member = place[0], place[1]
    rows, width = in_eigs.shape[1], basis.shape[-1]
    steps = basis.shape[0] * 2
    copies = []
    for k in range(steps):
        y, zs = k // 2, pl.ds(k % 2 * 4, 4)
        copies.append(
            [
                pltpu.make_async_copy(src.at[zs, y], basis.at[y, zs, at], sems.at[2 * k + side])
                for side, (src, at) in enumerate(((own, core), (other, 1 - core)))
            ]
        )
    for pair in copies:
        for copy in pair:
            copy.start()

    def block(k):
        return basis[k // 2, k % 2 * 4 : k % 2 * 4 + 4].reshape(rows, width)

    projected = jnp.zeros((grad.shape[0], width), jnp.float32)
    for k in range(steps):
        for copy in copies[k]:
            copy.wait()
        projected += jnp.dot(
            grad[:, k * rows : (k + 1) * rows], block(k), preferred_element_type=jnp.float32
        )
    denominator = out_eigs[...] * in_eigs[...] + DAMPING
    scaled = (projected / denominator).astype(jnp.bfloat16)
    sent = []
    for k in range(steps):
        share = lax.dot_general(
            scaled, block(k), (((1,), (1,)), ((), ())), preferred_element_type=jnp.float32
        )

        @pl.when(member == k)
        def _():
            kept[...] = share

        staged[k] = jnp.where(member == k, 0.0, share).astype(staged.dtype)
        sent.append(pltpu.make_async_copy(staged.at[k], terms.at[k], sems.at[2 * steps + k]))
        sent[k].start()
    for copy in sent:
        copy.wait()


def precondition(own, other, grad, in_eigs, out_eigs):
    place = jnp.stack([lax.axis_index("core"), lax.axis_index(GROUP)]).astype(jnp.int32)
    rows = grad.shape[0]
    width = in_eigs.shape[0]
    hbm = pl.BlockSpec(memory_space=pltpu.HBM)
    vmem = pl.BlockSpec(memory_space=pltpu.VMEM)
    return pl.pallas_call(
        precondition_kernel,
        out_shape=(
            jax.ShapeDtypeStruct((8, rows, width), jnp.bfloat16),
            jax.ShapeDtypeStruct((rows, width), jnp.float32),
        ),
        in_specs=[pl.BlockSpec(memory_space=pltpu.SMEM), hbm, hbm, vmem, vmem, vmem],
        out_specs=(hbm, vmem),
        scratch_shapes=[
            pltpu.VMEM((4, 8, 2, rows, width), jnp.bfloat16),
            pltpu.VMEM((8, rows, width), jnp.bfloat16),
            pltpu.SemaphoreType.DMA((24,)),
        ],
        compiler_params=pltpu.CompilerParams(vmem_limit_bytes=50 << 20),
        cost_estimate=pl.CostEstimate(
            flops=4 * rows * 8 * width * width, bytes_accessed=24 * width * width, transcendentals=0
        ),
    )(place, own, other, grad, in_eigs[None, :], out_eigs[:, None])


def shards(activations, out_grads, counts, owners, rotated_grad, basis, input_eigs, output_eigs):
    slots, width = activations.shape
    owned_width = basis.shape[0]
    blocks_per = width // owned_width
    group_count = lax.axis_size("yl") * lax.axis_size("x")
    is_live = lax.broadcasted_iota(jnp.int32, (slots, 1), 0) < counts[0]
    kept_out = jnp.where(is_live, out_grads, jnp.zeros_like(out_grads))
    joined = jnp.concatenate([basis, activations])
    row = lax.broadcasted_iota(jnp.int32, (joined.shape[0], 1), 0)
    joined = jnp.where(row < owned_width + counts[0], joined, jnp.zeros_like(joined))
    owner_pair = [
        (lax.rem(idx, blocks_per) * owned_width, lax.div(idx, blocks_per))
        for idx in (owners[0], shift(owners, "core", 1)[0])
    ]
    column, kept_out, owner_pair = lax.optimization_barrier(
        (spread(joined, "yh"), kept_out, owner_pair)
    )
    own = lax.all_gather(column[:, :owned_width], "z", axis=0)
    kept_in, kept_out = lax.optimization_barrier((column[:, owned_width:], spread(kept_out, "z")))
    kept_out = spread(kept_out.reshape(-1, width), "yh").reshape(-1, width)
    kept_in = lax.all_gather(kept_in.reshape(-1, width), "z", axis=0, tiled=True)
    pieces = []
    for offset, _ in owner_pair:
        columns = [lax.dynamic_slice_in_dim(v, offset, owned_width, 1) for v in (kept_in, kept_out)]
        pieces.append(jnp.concatenate(columns).reshape(group_count, -1, owned_width))
    arrived = lax.all_to_all(jnp.concatenate(pieces, axis=1), GROUP, 0, 0, tiled=True)
    rows = pieces[0].shape[1]
    piece, for_other = (
        lax.dynamic_slice(arrived, (root, k * rows, 0), (1, rows, owned_width))[0]
        for k, (_, root) in enumerate(owner_pair)
    )
    theirs = shift(jnp.stack([kept_in, kept_out]), "core", 1)
    own, piece, for_other, theirs = lax.optimization_barrier((own, piece, for_other, theirs))
    core = lax.axis_index("core")
    shares = jnp.stack([jnp.where(core == k, piece, for_other) for k in range(2)])
    shares = jnp.broadcast_to(shares[:, None], (2, group_count) + piece.shape)
    owned = lax.all_to_all(
        shares.reshape((-1,) + piece.shape), ("core",) + GROUP, 0, 0, tiled=True
    ).reshape(2, 2, -1, owned_width)
    owned_mine, owned_theirs = (
        lax.dynamic_index_in_dim(owned, k, 0, keepdims=False) for k in (core, 1 - core)
    )
    contract_rows = (((0,), (0,)), ((), ()))
    cov_in, cov_out = (
        (
            lax.dot_general(mine, owned_mine[k], contract_rows, preferred_element_type=jnp.float32)
            + lax.dot_general(theirs[k], owned_theirs[k], contract_rows, preferred_element_type=jnp.float32)
        )
        / jnp.float32(SAMPLED)
        for k, mine in enumerate((kept_in, kept_out))
    )

    other = shift(own, "core", 1)
    terms, own_term = precondition(own, other, rotated_grad, input_eigs, output_eigs)
    terms = lax.all_to_all(terms, GROUP, 0, 0, tiled=True)
    preconditioned = own_term
    for k in range(group_count):
        preconditioned += terms[k].astype(jnp.float32)
    return (cov_in, cov_out, preconditioned)


def solution(mesh):
    devices = mesh.devices.reshape(4, 8, 2, 2, 4)
    fine = Mesh(devices, DP + GROUP)
    placed = (
        P(DP, GROUP),
        P(DP, GROUP),
        P(DP),
        P(DP),
        P(DP, None),
        P(DP, GROUP),
        P(GROUP),
        P(DP),
    )
    return jax.shard_map(
        shards,
        mesh=fine,
        in_specs=placed,
        out_specs=(P(GROUP, DP), P(GROUP, DP), P(DP, GROUP)),
        check_vma=False,
    )
```

```python
import jax
import jax.numpy as jnp
from jax import lax
from jax.experimental import pallas as pl
from jax.experimental.pallas import tpu as pltpu
from jax.sharding import Mesh, PartitionSpec as P

DAMPING = 0.1
SAMPLED = 768
DP = ("yh", "z", "core")
GROUP = ("yl", "x")


def shift(value, axis, by):
    size = lax.axis_size(axis)
    return lax.ppermute(value, axis, [((i + by) % size, i) for i in range(size)])


def spread(block, axis):
    size = lax.axis_size(axis)
    return lax.all_to_all(jnp.broadcast_to(block[None], (size,) + block.shape), axis, 0, 0, tiled=True)


def precondition_kernel(place, own, other, grad, in_eigs, out_eigs, terms, kept, basis, sems):
    core, member = place[0], place[1]
    rows, width = in_eigs.shape[1], basis.shape[-1]
    steps = basis.shape[0] * 2
    copies = []
    for k in range(steps):
        y, zs = k // 2, pl.ds(k % 2 * 4, 4)
        copies.append(
            [
                pltpu.make_async_copy(src.at[zs, y], basis.at[y, zs, at], sems.at[2 * k + side])
                for side, (src, at) in enumerate(((own, core), (other, 1 - core)))
            ]
        )
    for pair in copies:
        for copy in pair:
            copy.start()

    def block(k):
        return basis[k // 2, k % 2 * 4 : k % 2 * 4 + 4].reshape(rows, width)

    projected = jnp.zeros((grad.shape[0], width), jnp.float32)
    for k in range(steps):
        for copy in copies[k]:
            copy.wait()
        projected += jnp.dot(
            grad[:, k * rows : (k + 1) * rows], block(k), preferred_element_type=jnp.float32
        )
    denominator = out_eigs[...] * in_eigs[...] + DAMPING
    scaled = (projected / denominator).astype(jnp.bfloat16)
    for k in range(steps):
        share = lax.dot_general(
            scaled, block(k), (((1,), (1,)), ((), ())), preferred_element_type=jnp.float32
        )

        @pl.when(member == k)
        def _():
            kept[...] = share

        terms[k] = jnp.where(member == k, 0.0, share).astype(terms.dtype)


def precondition(own, other, grad, in_eigs, out_eigs):
    place = jnp.stack([lax.axis_index("core"), lax.axis_index(GROUP)]).astype(jnp.int32)
    rows = grad.shape[0]
    width = in_eigs.shape[0]
    hbm = pl.BlockSpec(memory_space=pltpu.HBM)
    vmem = pl.BlockSpec(memory_space=pltpu.VMEM)
    return pl.pallas_call(
        precondition_kernel,
        out_shape=(
            jax.ShapeDtypeStruct((8, rows, width), jnp.bfloat16),
            jax.ShapeDtypeStruct((rows, width), jnp.float32),
        ),
        in_specs=[pl.BlockSpec(memory_space=pltpu.SMEM), hbm, hbm, vmem, vmem, vmem],
        out_specs=(vmem, vmem),
        scratch_shapes=[
            pltpu.VMEM((4, 8, 2, rows, width), jnp.bfloat16),
            pltpu.SemaphoreType.DMA((16,)),
        ],
        compiler_params=pltpu.CompilerParams(vmem_limit_bytes=50 << 20),
        cost_estimate=pl.CostEstimate(
            flops=4 * rows * 8 * width * width, bytes_accessed=24 * width * width, transcendentals=0
        ),
    )(place, own, other, grad, in_eigs[None, :], out_eigs[:, None])


def shards(activations, out_grads, counts, owners, rotated_grad, basis, input_eigs, output_eigs):
    slots, width = activations.shape
    owned_width = basis.shape[0]
    blocks_per = width // owned_width
    group_count = lax.axis_size("yl") * lax.axis_size("x")
    is_live = lax.broadcasted_iota(jnp.int32, (slots, 1), 0) < counts[0]
    kept_out = jnp.where(is_live, out_grads, jnp.zeros_like(out_grads))
    joined = jnp.concatenate([basis, activations])
    row = lax.broadcasted_iota(jnp.int32, (joined.shape[0], 1), 0)
    joined = jnp.where(row < owned_width + counts[0], joined, jnp.zeros_like(joined))
    owner_pair = [
        (lax.rem(idx, blocks_per) * owned_width, lax.div(idx, blocks_per))
        for idx in (owners[0], shift(owners, "core", 1)[0])
    ]
    column, kept_out, owner_pair = lax.optimization_barrier(
        (spread(joined, "yh"), kept_out, owner_pair)
    )
    own = lax.all_gather(column[:, :owned_width], "z", axis=0)
    kept_in, kept_out = lax.optimization_barrier((column[:, owned_width:], spread(kept_out, "z")))
    kept_out = spread(kept_out.reshape(-1, width), "yh").reshape(-1, width)
    kept_in = lax.all_gather(kept_in.reshape(-1, width), "z", axis=0, tiled=True)
    pieces = []
    for offset, _ in owner_pair:
        columns = [lax.dynamic_slice_in_dim(v, offset, owned_width, 1) for v in (kept_in, kept_out)]
        pieces.append(jnp.concatenate(columns).reshape(group_count, -1, owned_width))
    arrived = lax.all_to_all(jnp.concatenate(pieces, axis=1), GROUP, 0, 0, tiled=True)
    rows = pieces[0].shape[1]
    piece, for_other = (
        lax.dynamic_slice(arrived, (root, k * rows, 0), (1, rows, owned_width))[0]
        for k, (_, root) in enumerate(owner_pair)
    )
    theirs = shift(jnp.stack([kept_in, kept_out]), "core", 1)
    own, piece, for_other, theirs = lax.optimization_barrier((own, piece, for_other, theirs))
    core = lax.axis_index("core")
    shares = jnp.stack([jnp.where(core == k, piece, for_other) for k in range(2)])
    shares = jnp.broadcast_to(shares[:, None], (2, group_count) + piece.shape)
    owned = lax.all_to_all(
        shares.reshape((-1,) + piece.shape), ("core",) + GROUP, 0, 0, tiled=True
    ).reshape(2, 2, -1, owned_width)
    owned_mine, owned_theirs = (
        lax.dynamic_index_in_dim(owned, k, 0, keepdims=False) for k in (core, 1 - core)
    )
    contract_rows = (((0,), (0,)), ((), ()))
    cov_in, cov_out = (
        (
            lax.dot_general(mine, owned_mine[k], contract_rows, preferred_element_type=jnp.float32)
            + lax.dot_general(theirs[k], owned_theirs[k], contract_rows, preferred_element_type=jnp.float32)
        )
        / jnp.float32(SAMPLED)
        for k, mine in enumerate((kept_in, kept_out))
    )

    other = shift(own, "core", 1)
    terms, own_term = precondition(own, other, rotated_grad, input_eigs, output_eigs)
    terms = lax.all_to_all(terms, GROUP, 0, 0, tiled=True)
    preconditioned = own_term
    for k in range(group_count):
        preconditioned += terms[k].astype(jnp.float32)
    return (cov_in, cov_out, preconditioned)


def solution(mesh):
    devices = mesh.devices.reshape(4, 8, 2, 2, 4)
    fine = Mesh(devices, DP + GROUP)
    placed = (
        P(DP, GROUP),
        P(DP, GROUP),
        P(DP),
        P(DP),
        P(DP, None),
        P(DP, GROUP),
        P(GROUP),
        P(DP),
    )
    return jax.shard_map(
        shards,
        mesh=fine,
        in_specs=placed,
        out_specs=(P(GROUP, DP), P(GROUP, DP), P(DP, GROUP)),
        check_vma=False,
    )
```
